256 devices in a mesh: replica: 8 (over x, core), group: 32 (over z, y).
Axes of the slice: x: 4, y: 4, z: 8, core: 2. Of those that a mesh axis runs over, the one named last changes fastest.
Arguments:
- token_values: bfloat16 [10240, 7168], P(('replica', 'group')), parts along dimension 0, may hold values from -6 to 6
- token_scales: bfloat16 [10240, 56], P(('replica', 'group')), parts along dimension 0, may hold values from 0.25 to 4
- counts: int32 [256], P('replica'), parts along dimension 0, may hold values from 1 to 40, 768 in all
- gate_values: bfloat16 [9216, 7168], P('group'), may hold values from -0.0625 to 0.0625
- gate_scales: float32 [9216, 56], P('group'), may hold values from 0.5 to 2
- up_values: bfloat16 [9216, 7168], P('group'), may hold values from -0.0625 to 0.0625
- up_scales: float32 [9216, 56], P('group'), may hold values from 0.5 to 2
- down_values: bfloat16 [9216, 3584], P('group'), may hold values from -0.0625 to 0.0625
- down_scales: float32 [9216, 28], P('group'), may hold values from 0.5 to 2
Outputs:
- mixed: bfloat16 [10240, 3584], P(('replica', 'group')), parts along dimension 0
The draws below stay inside these ranges and needn't reach their ends.
There are 8 independent parts, one for each index of `replica`. The reference program is written for one: setup_inputs(seed, part) draws one part's arguments, and reference() takes and returns one part's arrays. A program takes and returns all parts, laid end to end along the dimension named above; an argument that names none is the same for every part. Nothing has to cross between parts.
Inputs may be any that keep to these rules, and one draw needn't show every extreme that they name: Device i's live tokens are its first counts[i] slots; the counts of a part sum to 768 and some device has exactly 40.
All inputs are finite; a program needn't handle non-finite values.
Results may differ from the reference program's by a relative error of at most 0.02.
Values may be sent and summed in bfloat16 or wider, within the bound.
A program may use at most 192 MiB of HBM per device.

```python
import math
import jax
import jax.numpy as jnp
import numpy as np
from jax import lax

D = 7168
FF = 9216
D_OUT = 3584
BLK = 128
ROWS = 24
CAP = 40
SLOTS = 1280
N_GROUP = 32


def shard_levels(own_key, dims, shards, least, largest):
    gain = 1.0
    for dim, shards_of in shards:
        steps = jax.random.uniform(jax.random.fold_in(jax.random.fold_in(own_key, 6), dim), (shards_of,), jnp.float32, least / len(shards), largest / len(shards))
        gain = gain * jnp.repeat(jnp.exp(steps), dims[dim] // shards_of).reshape((-1,) + (1,) * (len(dims) - 1 - dim))
    return gain


def length_profile(count, total, bound, lean):
    portions = [(1 << 20) // math.isqrt(grade ** lean) + 1 for grade in range(2, count + 1)]
    rest, given = total - bound - (count - 1), [1] * (count - 1)
    while rest > 0:
        free = [i for i in range(count - 1) if given[i] < bound]
        pool, remaining = sum([portions[i] for i in free]), rest
        for i in free:
            more = min(bound - given[i], max(1, remaining * portions[i] // pool), rest)
            given[i] = given[i] + more
            rest = rest - more
    return np.array([bound] + given)


def uneven(rng, count, total, most, slope):
    if count == 2:
        one = jax.random.randint(rng, (), max(1, total - most), min(most, total - 1) + 1)
        return jnp.stack([one, total - one])
    sizes = jnp.asarray(length_profile(count, total, most, slope), jnp.int32)
    couples = (count - 1) // 2
    giver, receiver = sizes[1:1 + 2 * couples:2], sizes[2:2 + 2 * couples:2]
    margin = jnp.minimum(giver - 1, most - receiver)
    passed = jax.random.randint(jax.random.fold_in(rng, 1), (couples,), 0, 1 << 20) % (margin + 1)
    sizes = sizes.at[1:1 + 2 * couples:2].set(giver - passed).at[2:2 + 2 * couples:2].set(receiver + passed)
    return sizes[jax.random.permutation(jax.random.fold_in(rng, 2), count)]


def bell_draw(key, extent, width, most, cuts=(), kind=jnp.bfloat16):
    level = shard_levels(key, extent, cuts, -0.22, 0.18) if cuts else 1.0
    values = jax.random.normal(key, extent, jnp.float32) * width * level
    return jnp.minimum(jnp.maximum(values, -most), most).astype(kind)


def setup_inputs(seed: int = 0, part: int = 0) -> dict:
    splits = jax.random.split(jax.random.key(seed), 10)
    part_splits = jax.random.split(jax.random.fold_in(splits[9], part), 10)
    return {
        "token_values": bell_draw(part_splits[0], (SLOTS, D), 1.0, 6.0, ((0, 32),)),
        "token_scales": jnp.clip(jnp.exp(math.log(4.0) - 2.7725887 * jax.random.uniform(part_splits[1], (SLOTS, D // BLK), jnp.float32) ** shard_levels(part_splits[1], (SLOTS, D // BLK), ((0, 32),), -0.2, 0.2)), 0.25, 4.0).astype(jnp.bfloat16),
        "counts": uneven(part_splits[2], N_GROUP, ROWS * N_GROUP, CAP, 2).astype(jnp.int32),
        "gate_values": bell_draw(splits[3], (FF, D), D ** -0.5, 0.0625, ((0, 32),)),
        "gate_scales": jnp.clip(jnp.exp(math.log(2.0) - 1.3862944 * jax.random.uniform(splits[4], (FF, D // BLK), jnp.float32) ** shard_levels(splits[4], (FF, D // BLK), ((0, 32),), -0.2, 0.2)), 0.5, 2.0),
        "up_values": bell_draw(splits[5], (FF, D), D ** -0.5, 0.0625, ((0, 32),)),
        "up_scales": jnp.clip(jnp.exp(math.log(2.0) - 1.3862944 * jax.random.uniform(splits[6], (FF, D // BLK), jnp.float32) ** shard_levels(splits[6], (FF, D // BLK), ((0, 32),), -0.2, 0.2)), 0.5, 2.0),
        "down_values": bell_draw(splits[7], (FF, D_OUT), FF ** -0.5, 0.0625, ((0, 32),)),
        "down_scales": jnp.clip(jnp.exp(math.log(2.0) - 1.3862944 * jax.random.uniform(splits[8], (FF, D_OUT // BLK), jnp.float32) ** shard_levels(splits[8], (FF, D_OUT // BLK), ((0, 32),), -0.2, 0.2)), 0.5, 2.0),
    }


def dequant(values, scales):
    row_count, feat_width = values.shape
    blocks = scales.shape[1]
    expanded = values.astype(jnp.float32).reshape(row_count, blocks, feat_width // blocks) * scales.astype(jnp.float32)[:, :, None]
    return expanded.reshape(row_count, feat_width).astype(jnp.bfloat16)


def reference(token_values, token_scales, counts, gate_values, gate_scales, up_values, up_scales, down_values, down_scales):
    token_rows = dequant(token_values, token_scales)
    w_gate = dequant(gate_values, gate_scales)
    w_up = dequant(up_values, up_scales)
    w_down = dequant(down_values, down_scales)
    contract = (((1,), (1,)), ((), ()))
    gate_act = lax.dot_general(token_rows, w_gate, contract, preferred_element_type=jnp.float32)
    up_act = lax.dot_general(token_rows, w_up, contract, preferred_element_type=jnp.float32)
    hidden = (jax.nn.silu(gate_act) * up_act).astype(jnp.bfloat16)
    unit_share = FF // N_GROUP
    hidden_blocks = hidden.reshape(SLOTS, N_GROUP, unit_share).transpose(1, 0, 2)
    down_blocks = w_down.reshape(N_GROUP, unit_share, D_OUT)

    def add_block(running, operands):
        partial_value = jnp.dot(operands[0], operands[1], preferred_element_type=jnp.float32).astype(jnp.bfloat16)
        partial_value = lax.optimization_barrier(partial_value)
        return running + partial_value.astype(jnp.float32), None

    running, _ = lax.scan(add_block, jnp.zeros((SLOTS, D_OUT), jnp.float32), (hidden_blocks, down_blocks))
    position = jnp.arange(SLOTS, dtype=jnp.int32)
    owner_of = position // CAP
    within = position % CAP
    live_mask = within < counts[owner_of]
    return jnp.where(live_mask[:, None], running, jnp.float32(0.0)).astype(jnp.bfloat16)
```

```python
import jax
import jax.numpy as jnp
from jax import lax
from jax.experimental import pallas as pl
from jax.experimental.pallas import tpu as pltpu
from jax.sharding import PartitionSpec as P

F32, BF16, I32 = jnp.float32, jnp.bfloat16, jnp.int32
N, NZ, NY = 32, 8, 4
CAP, LIVE = 40, 768
D, DO, FF = 7168, 3584, 288
HOLD = 28
PW, OW = 256, 128
HALF = LIVE // 2
NSUB = 4
SUB = HALF // NSUB
STEPS = N // 2
FP = 384
T1 = 480
T2 = LIVE - T1
H1, H2 = T1 // 2, T2 // 2
OROW = 48
ORDER = (4, 3, -3, 2, -2, 1, -1, 0)


def kernel(
    counts, tv_h, ts_h, gv_h, gs_h, uv_h, us_h, dv_h, ds_h, out,
    tv, ts, gv, gs, uv, us, dv, ds, asrc, adst, xs, onehot, back, w, wd, acc, hid, ring,
    r1, r2, yz, zr, tz, ty1, ty2, res, osrc, odst,
    ld, a_s, a_r, g_s, g_r, s1, q1, s2, q2, sz, qz, st, qt, sy1, qy1, sy2, qy2, o_s, o_r,
):
    rep = lax.axis_index("replica")
    g = lax.axis_index("group")
    z, y = g // NY, g % NY
    up_y, dn_y = z * NY + (y + 1) % NY, z * NY + (y + 3) % NY
    up_z, dn_z = ((z + 1) % NZ) * NY + y, ((z + 7) % NZ) * NY + y
    is_holder = g < HOLD

    def remote(src, dst, send, recv, to):
        return pltpu.make_async_remote_copy(
            src, dst, send, recv, device_id=(rep, to), device_id_type=pl.DeviceIdType.MESH
        )

    loads = [
        pltpu.make_async_copy(a, b, ld.at[i])
        for i, (a, b) in enumerate(
            ((tv_h, tv), (ts_h, ts), (gv_h, gv), (gs_h, gs), (uv_h, uv), (us_h, us), (dv_h, dv), (ds_h, ds))
        )
    ]
    for load in loads:
        load.start()
    barrier = pltpu.get_barrier_semaphore()

    def greet(i, c):
        pl.semaphore_signal(barrier, inc=1, device_id=(rep, (g + i) % N), device_id_type=pl.DeviceIdType.MESH)
        return c

    lax.fori_loop(1, N, greet, 0)

    loads[0].wait()
    loads[1].wait()
    tsf = ts[...].astype(F32)
    for p in range(HOLD):
        lo = tv[:, PW * p : PW * p + 128].astype(F32) * tsf[:, 2 * p : 2 * p + 1]
        hi = tv[:, PW * p + 128 : PW * p + 256].astype(F32) * tsf[:, 2 * p + 1 : 2 * p + 2]
        asrc[p] = jnp.concatenate([lo, hi], axis=0).astype(BF16)
    pl.semaphore_wait(barrier, N - 1)

    def scatter(i, c):
        to = (g + i) % N

        @pl.when(to < HOLD)
        def _():
            remote(asrc.at[to], adst.at[g], a_s, a_r, to).start()

        return c

    lax.fori_loop(1, N, scatter, 0)

    offs, off = [], jnp.int32(0)
    lane = lax.broadcasted_iota(I32, (16, N * CAP), 1)
    target = jnp.full((16, N * CAP), -1, I32)
    for i in range(N):
        c = counts[i]
        rel = lane - CAP * i
        target = jnp.where((rel >= 0) & (rel < c), rel + off, target)
        offs.append(off)
        off = off + c
    row16 = lax.broadcasted_iota(I32, (16, N * CAP), 0)

    def build(r, c):
        hit = target == row16 + r * 16
        onehot[pl.ds(pl.multiple_of(r * 16, 16), 16), :] = jnp.where(hit, 1.0, 0.0).astype(BF16)
        return c

    lax.fori_loop(0, LIVE // 16, build, 0)

    for v, s, at in ((gv, gs, 0), (uv, us, FP)):
        loads[2 if at == 0 else 4].wait()
        loads[3 if at == 0 else 5].wait()

        def deq(r, c, v=v, s=s, at=at):
            r0 = pl.multiple_of(r * 32, 32)
            sf = s[pl.ds(r0, 32), :]
            for b in range(D // 128):
                val = v[pl.ds(r0, 32), 128 * b : 128 * b + 128].astype(F32) * sf[:, b : b + 1]
                w[b // 2, pl.ds(at + r0, 32), 128 * (b % 2) : 128 * (b % 2) + 128] = val.astype(BF16)
            return c

        lax.fori_loop(0, FF // 32, deq, 0)

    def pad(p, c):
        w[p, FF:FP, :] = jnp.zeros((FP - FF, PW), BF16)
        w[p, FP + FF :, :] = jnp.zeros((FP - FF, PW), BF16)
        return c

    lax.fori_loop(0, HOLD, pad, 0)
    acc[...] = jnp.zeros_like(acc)

    @pl.when(is_holder)
    def _():
        adst[g] = asrc[g]
        pltpu.make_async_copy(adst.at[pl.ds(0, N - 1)], adst.at[pl.ds(0, N - 1)], a_r).wait()

        def spread(k, c):
            a = adst[2 * k].astype(F32)
            b = adst[2 * k + 1].astype(F32)
            rows = pl.ds(pl.multiple_of(k * 80, 16), 80)
            xs[rows, 0:128] = jnp.concatenate([a[:CAP], b[:CAP]], axis=0).astype(BF16)
            xs[rows, 128:256] = jnp.concatenate([a[CAP:], b[CAP:]], axis=0).astype(BF16)
            return c

        lax.fori_loop(0, N // 2, spread, 0)

    corner = (y + z) % NY
    nxt = (
        jnp.where(corner == 3, up_z, up_y),
        jnp.where(corner == 0, dn_z, dn_y),
        jnp.where(corner == 3, up_y, up_z),
        jnp.where(corner == 0, dn_y, dn_z),
    )
    turn = (z + 32 - 3 * y) % NZ
    pos_a = NY * z + corner
    pos_b = jnp.where(turn < 4, 4 * y + turn, 4 * (y + 4) + turn - 4)

    def source(q, d):
        p = ((pos_a if q < 2 else pos_b) + (64 - d if q % 2 == 0 else d)) % N
        hi, r = p // 4, p % 4
        if q < 2:
            return hi * NY + (r + 8 - hi) % NY
        return ((3 * hi + r) % NZ) * NY + hi % NY

    def last(q, u):
        return (u < NSUB // 2) == (q % 2 == 0)

    def piece(q, u, src):
        return ring.at[src, pl.ds((q // 2) * HALF + u * SUB, SUB), :]

    def forward(q, u, src, d):
        ref = piece(q, u, src)
        return remote(ref, ref, g_s.at[q, d], g_r.at[q, u, d], nxt[q])

    def multiply(src, r0, n):
        acc[pl.ds(r0, n), :] += lax.dot_general(
            ring[src, pl.ds(r0, n), :], w[src], (((1,), (1,)), ((), ())), preferred_element_type=F32
        )

    @pl.when(is_holder)
    def _():
        for h in range(2):
            ring[g, pl.ds(h * HALF, HALF), :] = jnp.dot(
                onehot[pl.ds(h * HALF, HALF), :], xs[...], preferred_element_type=F32
            ).astype(BF16)
            for u in range(NSUB):
                for q in (2 * h, 2 * h + 1):
                    forward(q, u, g, 0).start()
        multiply(g, 0, HALF)
        multiply(g, HALF, HALF)

    loads[6].wait()
    loads[7].wait()

    def deq_down(r, c):
        r0 = pl.multiple_of(r * 32, 32)
        sf = ds[pl.ds(r0, 32), :]
        for b in range(HOLD):
            val = dv[pl.ds(r0, 32), 128 * b : 128 * b + 128].astype(F32) * sf[:, b : b + 1]
            wd[b % NY, pl.ds(r0, 32), 128 * (b // NY) : 128 * (b // NY) + 128] = val.astype(BF16)
        return c

    lax.fori_loop(0, FF // 32, deq_down, 0)
    wd[:, FF:, :] = jnp.zeros((NY, FP - FF, DO // NY), BF16)

    def gather(t, c):
        srcs = [source(q, t + 1) for q in range(4)]
        for u in range(NSUB):
            for q in range(4):

                @pl.when(srcs[q] < HOLD)
                def _(q=q, u=u):
                    forward(q, u, srcs[q], t).wait_recv()
                    if last(q, u):
                        forward(q, u, srcs[q], t + 1).start()
                    else:

                        @pl.when(t < STEPS - 2)
                        def _():
                            forward(q, u, srcs[q], t + 1).start()

        for q in range(4):

            @pl.when(srcs[q] < HOLD)
            def _(q=q):
                multiply(srcs[q], (q // 2) * HALF, HALF)

        return c

    lax.fori_loop(0, STEPS - 1, gather, 0)
    for q in range(4):
        src = source(q, STEPS)

        @pl.when(src < HOLD)
        def _(q=q, src=src):
            for u in range(NSUB):
                if last(q, u):
                    forward(q, u, src, STEPS - 1).wait_recv()
            multiply(src, (q // 2) * HALF + (q % 2) * (HALF // 2), HALF // 2)

    for r in range(LIVE // 128):
        rows = pl.ds(r * 128, 128)
        gate = acc[rows, 0:FP]
        hid[rows, :] = (gate / (1.0 + jnp.exp(-gate)) * acc[rows, FP : 2 * FP]).astype(BF16)

    def slab(dy):
        yy = (y + dy) % NY
        for r in range(4):
            rows = pl.ds(r * 192, 192)
            part = jnp.dot(hid[rows, :], wd[yy], preferred_element_type=F32).astype(BF16)
            for zp in range(7):
                w[zp * NY + yy, rows, 0:OW] = part[:, zp * OW : (zp + 1) * OW]

    def part(zp, dy, r0, n):
        return w.at[zp * NY + (y + dy) % NY, pl.ds(r0, n), 0:OW]

    def add(ref, r0, n, *others):
        total = ref[pl.ds(r0, n), :].astype(F32)
        for other in others:
            total = total + other[...].astype(F32)
        return total

    zps = [(z + dz + 8) % NZ for dz in ORDER]

    def m1(k, up):
        if up:
            return remote(part(zps[k], 2, 0, H1), r1.at[0, k], s1.at[0, k], q1.at[0, k], up_y)
        return remote(part(zps[k], 2, H1, H1), r1.at[1, k], s1.at[1, k], q1.at[1, k], dn_y)

    def m2(k, up):
        if up:
            return remote(part(zps[k], 1, 0, T1), r2.at[0, k], s2.at[0, k], q2.at[0, k], up_y)
        return remote(part(zps[k], 3, 0, T1), r2.at[1, k], s2.at[1, k], q2.at[1, k], dn_y)

    def mz(k, way, dist):
        to = up_z if way == 0 else dn_z
        if dist == 4:
            rows = pl.ds(way * H1, H1)
            return remote(yz.at[k, rows, :], zr.at[way, 3, rows, :], sz.at[way, 3], qz.at[way, 3], to)
        return remote(yz.at[k], zr.at[way, dist - 1], sz.at[way, dist - 1], qz.at[way, dist - 1], to)

    def mt(k, way, dist, yp):
        to = up_z if way == 0 else dn_z
        p = zps[k] * NY + yp
        if dist == 4:
            src = w.at[p, pl.ds(T1 + way * H2, H2), 0:OW]
            dst = tz.at[way, 3, yp, pl.ds(way * H2, H2), :]
            return remote(src, dst, st.at[way, 3, yp], qt.at[way, 3, yp], to)
        src = w.at[p, pl.ds(T1, T2), 0:OW]
        return remote(src, tz.at[way, dist - 1, yp], st.at[way, dist - 1, yp], qt.at[way, dist - 1, yp], to)

    def my1(up):
        if up:
            return remote(part(z, 2, T1, H2), ty1.at[0], sy1.at[0], qy1.at[0], up_y)
        return remote(part(z, 2, T1 + H2, H2), ty1.at[1], sy1.at[1], qy1.at[1], dn_y)

    def my2(up):
        if up:
            return remote(part(z, 1, T1, T2), ty2.at[0], sy2.at[0], qy2.at[0], up_y)
        return remote(part(z, 3, T1, T2), ty2.at[1], sy2.at[1], qy2.at[1], dn_y)

    def guarded(k, f):
        pl.when(zps[k] < 7)(f)

    def second(k):
        def f():
            for way in range(2):
                m1(k, way == 0).wait_recv()
                ref = part(zps[k], 1 if way == 0 else 3, way * H1, H1)
                ref[...] = (ref[...].astype(F32) + r1[way, k].astype(F32)).astype(BF16)
                m2(k, way == 0).start()

        guarded(k, f)

    def line(k):
        dz = ORDER[k]

        def f():
            m2(k, True).wait_recv()
            m2(k, False).wait_recv()
            ways = {4: (), 0: (0, 1)}.get(dz, (0,) if dz > 0 else (1,))
            for way in ways:
                mz(k, way, abs(dz) + 1).wait_recv()
            for h in range(2):
                rows = pl.ds(h * H1, H1)
                total = part(zps[k], 0, h * H1, H1)[...].astype(F32)
                total = total + r2[0, k, rows, :].astype(F32) + r2[1, k, rows, :].astype(F32)
                for way in ways:
                    if abs(dz) < 3 or way == h:
                        total = total + zr[way, abs(dz), rows, :].astype(F32)
                if dz == 0:
                    res[rows, :] = total.astype(BF16)
                else:
                    yz[k, rows, :] = total.astype(BF16)
            if dz == 4:
                mz(k, 0, 4).start()
                mz(k, 1, 4).start()
            elif dz != 0:
                mz(k, ways[0], abs(dz)).start()

        guarded(k, f)

    def plane(dist):
        if dist == 4:

            def f():
                for yp in range(NY):
                    mt(0, 0, 4, yp).start()
                    mt(0, 1, 4, yp).start()

            guarded(0, f)
            return
        if dist == 0:
            k = len(ORDER) - 1

            def f():
                for dy in (2, 1, 3, 0):
                    yp = (y + dy) % NY
                    mt(k, 0, 1, yp).wait_recv()
                    mt(k, 1, 1, yp).wait_recv()
                    ref = part(z, dy, T1, T2)
                    ref[...] = (ref[...].astype(F32) + tz[0, 0, yp].astype(F32) + tz[1, 0, yp].astype(F32)).astype(BF16)
                    if dy == 2:
                        my1(True).start()
                        my1(False).start()

            guarded(k, f)
            return
        for yp in range(NY):
            for way in range(2):
                k = ORDER.index(dist if way == 0 else -dist)

                def f(k=k, way=way, yp=yp):
                    mt(k, way, dist + 1, yp).wait_recv()
                    if dist == 3:
                        ref = w.at[zps[k] * NY + yp, pl.ds(T1 + way * H2, H2), 0:OW]
                        got = tz[way, 3, yp, pl.ds(way * H2, H2), :]
                    else:
                        ref = w.at[zps[k] * NY + yp, pl.ds(T1, T2), 0:OW]
                        got = tz[way, dist, yp]
                    ref[...] = (ref[...].astype(F32) + got.astype(F32)).astype(BF16)
                    mt(k, way, dist, yp).start()

                guarded(k, f)

    def cross():
        def f():
            for way in range(2):
                my1(way == 0).wait_recv()
                ref = part(z, 1 if way == 0 else 3, T1 + way * H2, H2)
                ref[...] = (ref[...].astype(F32) + ty1[way].astype(F32)).astype(BF16)
                my2(way == 0).start()

        pl.when(z < 7)(f)

    slab(2)
    for k in range(8):

        def f(k=k):
            m1(k, True).start()
            m1(k, False).start()

        guarded(k, f)
    slab(1)
    slab(3)
    slab(0)
    plane(4)
    second(0)
    second(1)
    plane(3)
    for k in range(2, 8):
        second(k)
    plane(2)
    line(0)
    plane(1)
    line(1)
    line(2)
    line(3)
    plane(0)
    line(4)
    cross()

    jrow = lax.broadcasted_iota(I32, (OROW, LIVE), 0)
    diff = lax.broadcasted_iota(I32, (OROW, LIVE), 1) - jrow
    for i in range(N):
        hit = (diff == offs[i]) & (jrow < counts[i])
        back[i * OROW : (i + 1) * OROW, :] = jnp.where(hit, 1.0, 0.0).astype(BF16)

    line(5)
    line(6)
    line(7)

    @pl.when(z < 7)
    def _():
        my2(True).wait_recv()
        my2(False).wait_recv()
        total = part(z, 0, T1, T2)[...].astype(F32) + ty2[0].astype(F32) + ty2[1].astype(F32)
        res[T1:, :] = total.astype(BF16)
        for h in range(4):
            slots = jnp.dot(back[h * 384 : (h + 1) * 384, :], res[...], preferred_element_type=F32).astype(BF16)
            for i in range(8):
                osrc[8 * h + i] = slots[i * OROW : (i + 1) * OROW]
        odst[g] = osrc[g]

        def give(i, c):
            to = (g + i) % N
            remote(osrc.at[to], odst.at[g], o_s, o_r, to).start()
            return c

        lax.fori_loop(1, N, give, 0)

    def drain(t, c):
        for q in range(4):

            @pl.when(source(q, t) < HOLD)
            def _(q=q):
                ref = ring.at[0, pl.ds(0, HALF), :]
                pltpu.make_async_copy(ref, ref, g_s.at[q, t]).wait()

        return c

    lax.fori_loop(0, STEPS - 1, drain, 0)
    for q in range(4):

        @pl.when(source(q, STEPS - 1) < HOLD)
        def _(q=q):
            ref = ring.at[0, pl.ds(0, HALF // 2), :]
            pltpu.make_async_copy(ref, ref, g_s.at[q, STEPS - 1]).wait()

    for k in range(8):

        def f(k=k):
            dz = ORDER[k]
            for way in range(2):
                m1(k, way == 0).wait_send()
                m2(k, way == 0).wait_send()
                if dz == 4 or (dz > 0 and way == 0) or (dz < 0 and way == 1):
                    mz(k, way, abs(dz)).wait_send()
                    for yp in range(NY):
                        mt(k, way, abs(dz), yp).wait_send()

        guarded(k, f)

    @pl.when(is_holder)
    def _():
        some = asrc.at[pl.ds(0, HOLD - 1)]
        pltpu.make_async_copy(some, some, a_s).wait()
        for way in range(2):
            my1(way == 0).wait_send()
            my2(way == 0).wait_send()
        some = odst.at[pl.ds(0, HOLD - 1)]
        pltpu.make_async_copy(some, some, o_r).wait()
        some = osrc.at[pl.ds(0, N - 1)]
        pltpu.make_async_copy(some, some, o_s).wait()

    @pl.when(g >= HOLD)
    def _():
        some = asrc.at[pl.ds(0, HOLD)]
        pltpu.make_async_copy(some, some, a_s).wait()
        some = odst.at[pl.ds(0, HOLD)]
        pltpu.make_async_copy(some, some, o_r).wait()

    for p in range(HOLD):
        out[:, p * OW : (p + 1) * OW] = odst[p][:CAP]


def shards(tv, ts, counts, gv, gs, uv, us, dv, ds):
    any_space = pl.BlockSpec(memory_space=pl.ANY)
    vmem, dma = pltpu.VMEM, pltpu.SemaphoreType.DMA
    return pl.pallas_call(
        kernel,
        out_shape=jax.ShapeDtypeStruct((CAP, DO), BF16),
        in_specs=[pl.BlockSpec(memory_space=pltpu.SMEM)] + [any_space] * 8,
        out_specs=pl.BlockSpec(memory_space=pltpu.VMEM),
        scratch_shapes=[
            vmem((CAP, D), BF16),
            vmem((CAP, D // 128), BF16),
            vmem((FF, D), BF16),
            vmem((FF, D // 128), F32),
            vmem((FF, D), BF16),
            vmem((FF, D // 128), F32),
            vmem((FF, DO), BF16),
            vmem((FF, DO // 128), F32),
            vmem((HOLD, 2 * CAP, 128), BF16),
            vmem((N, 2 * CAP, 128), BF16),
            vmem((N * CAP, PW), BF16),
            vmem((LIVE, N * CAP), BF16),
            vmem((N * OROW, LIVE), BF16),
            vmem((HOLD, 2 * FP, PW), BF16),
            vmem((NY, FP, DO // NY), BF16),
            vmem((LIVE, 2 * FP), F32),
            vmem((LIVE, FP), BF16),
            vmem((HOLD, LIVE, PW), BF16),
            vmem((2, 8, H1, OW), BF16),
            vmem((2, 8, T1, OW), BF16),
            vmem((8, T1, OW), BF16),
            vmem((2, 4, T1, OW), BF16),
            vmem((2, 4, NY, T2, OW), BF16),
            vmem((2, H2, OW), BF16),
            vmem((2, T2, OW), BF16),
            vmem((LIVE, OW), BF16),
            vmem((N, OROW, OW), BF16),
            vmem((HOLD, OROW, OW), BF16),
            dma((8,)),
            dma,
            dma,
            dma((4, STEPS)),
            dma((4, NSUB, STEPS)),
            dma((2, 8)),
            dma((2, 8)),
            dma((2, 8)),
            dma((2, 8)),
            dma((2, 4)),
            dma((2, 4)),
            dma((2, 4, NY)),
            dma((2, 4, NY)),
            dma((2,)),
            dma((2,)),
            dma((2,)),
            dma((2,)),
            dma,
            dma,
        ],
        compiler_params=pltpu.CompilerParams(
            collective_id=0, has_side_effects=True, vmem_limit_bytes=60 * 2**20
        ),
        cost_estimate=pl.CostEstimate(flops=10**10, bytes_accessed=12 * 10**6, transcendentals=LIVE * FF),
        name="swiglu",
    )(counts, tv, ts, gv, gs, uv, us, dv, ds)


def solution(mesh):
    rows, split = P(("replica", "group"), None), P("group", None)
    in_specs = (rows, rows, P("replica")) + (split,) * 6
    return jax.shard_map(shards, mesh=mesh, in_specs=in_specs, out_specs=rows, check_vma=False)
```

```python
import jax
import jax.numpy as jnp
from jax import lax
from jax.experimental import pallas as pl
from jax.experimental.pallas import tpu as pltpu
from jax.sharding import PartitionSpec as P

F32, BF16, I32 = jnp.float32, jnp.bfloat16, jnp.int32
N, NZ, NY = 32, 8, 4
CAP, LIVE = 40, 768
D, DO, FF = 7168, 3584, 288
HOLD = 28
PW, OW = 256, 128
HALF = LIVE // 2
FP = 384
T1 = 480
T2 = LIVE - T1
H1, H2 = T1 // 2, T2 // 2
OROW = 48
ORDER = (4, 3, -3, 2, -2, 1, -1, 0)

ARRIVALS = (
    ("z1", 0, 0, 0), ("z1", 1, 0, 1), ("y2", 0, 0), ("y2", 1, 0), ("z1", 0, 0, 1), ("z1", 1, 0, 0),
    ("y1", 0, 0, 0, 0), ("y1", 1, 0, 0, 1), ("y1", 0, 0, 0, 1), ("y1", 1, 0, 0, 0), ("z2", 0, 0, 0), ("z2", 1, 0, 0),
    ("y1", 0, -1, 0, 0), ("y1", 1, -1, 0, 0), ("z1", 0, 1, 0), ("z1", 1, 1, 1), ("y1", 0, 1, 0, 1),
    ("y1", 1, 1, 0, 1), ("z2", 0, 0, 3), ("z2", 1, 0, 3), ("y2", 0, 1), ("y2", 1, 1), ("z2", 0, 0, 1),
    ("z2", 1, 0, 1), ("y1", 0, -1, 0, 1), ("y1", 1, -1, 0, 1), ("z1", 0, 1, 1), ("z1", 1, 1, 0), ("y1", 0, 1, 0, 0),
    ("y1", 1, 1, 0, 0), ("y1", 0, 0, 1, 0), ("y1", 1, 0, 1, 1), ("z2", 0, 1, 0), ("z2", 1, 1, 0), ("y1", 0, -1, 1, 0),
    ("y1", 1, -2, 0, 0), ("z1", 0, 2, 0), ("z1", 1, 2, 1), ("y1", 0, -2, 0, 0), ("y1", 1, 2, 0, 1), ("z2", 0, 1, 3),
    ("z2", 1, 1, 3), ("y1", 0, 2, 0, 1), ("y1", 1, 1, 1, 1), ("z2", 0, 0, 2), ("z2", 1, 0, 2), ("y1", 0, -2, 0, 1),
    ("y1", 1, -1, 1, 1), ("z2", 0, 1, 1), ("z2", 1, 1, 1), ("y1", 0, 2, 0, 0), ("y1", 1, -2, 0, 1), ("z1", 0, 2, 1),
    ("z1", 1, 2, 0), ("y1", 0, 1, 1, 0), ("y1", 1, 2, 0, 0), ("z2", 0, 2, 0), ("z2", 1, 2, 0), ("y1", 0, -3, 0, 0),
    ("y1", 1, -3, 0, 0), ("z1", 0, 3, 0), ("z1", 1, 3, 1), ("y1", 0, 3, 0, 1), ("y1", 1, 3, 0, 1),
    ("y1", 0, -2, 1, 0), ("y1", 1, 2, 1, 1), ("z2", 0, 2, 3), ("z2", 1, 2, 3), ("y1", 0, 2, 1, 0),
    ("y1", 1, -2, 1, 1), ("z2", 0, 1, 2), ("z2", 1, 1, 2), ("y1", 0, -3, 0, 1), ("y1", 1, -3, 0, 1), ("z2", 0, 2, 1),
    ("z2", 1, 2, 1), ("y1", 0, 3, 0, 0), ("y1", 1, 3, 0, 0), ("z2", 0, 3, 0), ("z2", 1, 3, 0), ("z2", 0, 3, 3),
    ("z2", 1, 3, 3), ("y1", 0, -3, 1, 0), ("y1", 1, 4, 0, 0), ("z2", 0, 2, 2), ("z2", 1, 2, 2), ("y1", 0, 4, 0, 0),
    ("y1", 1, 4, 0, 1), ("z2", 0, 3, 1), ("z2", 1, 3, 1), ("y1", 0, 4, 0, 1), ("y1", 1, 3, 1, 1), ("z2", 0, 3, 2),
    ("z2", 1, 3, 2), ("y1", 0, 3, 1, 0), ("y1", 1, -3, 1, 1), ("y1", 0, 4, 1, 0), ("y1", 1, 4, 1, 1),
)


def kernel(
    counts, tv_h, ts_h, gv_h, gs_h, uv_h, us_h, dv_h, ds_h, out,
    tv, ts, gv, gs, gst, uv, us, ust, dv, ds, dst, asrc, adst, xs, onehot, back, w, wd, acc, hid, ring,
    r1, r2, yz, zr, tz, ty1, ty2, res, osrc, odst,
    ld, a_s, a_r, z1_s, z1_r, y1_s, y1_r, y2_s, y2_r, z2_s, z2_r, s1, q1, s2, q2, sz, qz, st, qt, sy1, qy1, sy2, qy2, o_s, o_r,
):
    rep = lax.axis_index("replica")
    g = lax.axis_index("group")
    z, y = g // NY, g % NY
    up_y, dn_y = z * NY + (y + 1) % NY, z * NY + (y + 3) % NY
    up_z, dn_z = ((z + 1) % NZ) * NY + y, ((z + 7) % NZ) * NY + y
    def holds(dev):
        return dev % 9 != 0

    def piece_of(dev):
        return jnp.maximum(dev - 1 - dev // 9, 0)

    is_holder = holds(g)
    mine = piece_of(g)

    def remote(src, dst, send, recv, to):
        return pltpu.make_async_remote_copy(
            src, dst, send, recv, device_id=(rep, to), device_id_type=pl.DeviceIdType.MESH
        )

    loads = [
        pltpu.make_async_copy(a, b, ld.at[i])
        for i, (a, b) in enumerate(
            ((tv_h, tv), (ts_h, ts), (gv_h, gv), (gs_h, gst), (uv_h, uv), (us_h, ust), (dv_h, dv), (ds_h, dst))
        )
    ]
    for load in loads:
        load.start()
    barrier = pltpu.get_barrier_semaphore()

    def greet(i, c):
        pl.semaphore_signal(barrier, inc=1, device_id=(rep, (g + i) % N), device_id_type=pl.DeviceIdType.MESH)
        return c

    lax.fori_loop(1, N, greet, 0)

    loads[0].wait()
    loads[1].wait()
    tsf = ts[...].astype(F32)
    for p in range(HOLD):
        lo = tv[:, PW * p : PW * p + 128].astype(F32) * tsf[:, 2 * p : 2 * p + 1]
        hi = tv[:, PW * p + 128 : PW * p + 256].astype(F32) * tsf[:, 2 * p + 1 : 2 * p + 2]
        asrc[p] = jnp.concatenate([lo, hi], axis=0).astype(BF16)
    pl.semaphore_wait(barrier, N - 1)

    def scatter(i, c):
        to = (g + i) % N

        @pl.when(holds(to))
        def _():
            remote(asrc.at[piece_of(to)], adst.at[g], a_s, a_r, to).start()

        return c

    lax.fori_loop(1, N, scatter, 0)

    offs, off = [], jnp.int32(0)
    lane = lax.broadcasted_iota(I32, (16, N * CAP), 1)
    target = jnp.full((16, N * CAP), -1, I32)
    for i in range(N):
        c = counts[i]
        rel = lane - CAP * i
        target = jnp.where((rel >= 0) & (rel < c), rel + off, target)
        offs.append(off)
        off = off + c
    row16 = lax.broadcasted_iota(I32, (16, N * CAP), 0)

    def build(r, c):
        hit = target == row16 + r * 16
        onehot[pl.ds(pl.multiple_of(r * 16, 16), 16), :] = jnp.where(hit, 1.0, 0.0).astype(BF16)
        return c

    lax.fori_loop(0, LIVE // 16, build, 0)

    for v, s, st_, at in ((gv, gs, gst, 0), (uv, us, ust, FP)):
        loads[2 if at == 0 else 4].wait()
        loads[3 if at == 0 else 5].wait()
        s[...] = st_[...].T

        def deq(r, c, v=v, s=s, at=at):
            r0 = pl.multiple_of(r * 32, 32)
            sf = s[pl.ds(r0, 32), :]
            for b in range(D // 128):
                val = v[pl.ds(r0, 32), 128 * b : 128 * b + 128].astype(F32) * sf[:, b : b + 1]
                w[b // 2, pl.ds(at + r0, 32), 128 * (b % 2) : 128 * (b % 2) + 128] = val.astype(BF16)
            return c

        lax.fori_loop(0, FF // 32, deq, 0)

    loads[6].wait()
    loads[7].wait()
    ds[...] = dst[...].T

    def deq_down(r, c):
        r0 = pl.multiple_of(r * 32, 32)
        sf = ds[pl.ds(r0, 32), :]
        for b in range(HOLD):
            val = dv[pl.ds(r0, 32), 128 * b : 128 * b + 128].astype(F32) * sf[:, b : b + 1]
            wd[b % NY, pl.ds(r0, 32), 128 * (b // NY) : 128 * (b // NY) + 128] = val.astype(BF16)
        return c

    lax.fori_loop(0, FF // 32, deq_down, 0)
    wd[:, FF:, :] = jnp.zeros((NY, FP - FF, DO // NY), BF16)

    def pad(p, c):
        w[p, FF:FP, :] = jnp.zeros((FP - FF, PW), BF16)
        w[p, FP + FF :, :] = jnp.zeros((FP - FF, PW), BF16)
        return c

    lax.fori_loop(0, HOLD, pad, 0)
    acc[...] = jnp.zeros_like(acc)

    @pl.when(is_holder)
    def _():
        adst[g] = asrc[mine]
        pltpu.make_async_copy(adst.at[pl.ds(0, N - 1)], adst.at[pl.ds(0, N - 1)], a_r).wait()

        def spread(k, c):
            a = adst[2 * k].astype(F32)
            b = adst[2 * k + 1].astype(F32)
            rows = pl.ds(pl.multiple_of(k * 80, 16), 80)
            xs[rows, 0:128] = jnp.concatenate([a[:CAP], b[:CAP]], axis=0).astype(BF16)
            xs[rows, 128:256] = jnp.concatenate([a[CAP:], b[CAP:]], axis=0).astype(BF16)
            return c

        lax.fori_loop(0, N // 2, spread, 0)

    def multiply(src, r0, n):
        acc[r0 : r0 + n, :] += lax.dot_general(
            ring[src, r0 : r0 + n, :], w[src], (((1,), (1,)), ((), ())), preferred_element_type=F32
        )

    def at(dz, dy):
        dev = ((z + dz + 8) % NZ) * NY + (y + dy + 4) % NY
        return holds(dev), piece_of(dev)

    def when(dz, dy, f):
        live, p = at(dz, dy)
        pl.when(live)(lambda: f(p))

    to_z, to_y = (up_z, dn_z), (up_y, dn_y)

    def over(ref, sem):
        pltpu.make_async_copy(ref, ref, sem).wait()

    def gathered():
        for way in range(2):
            for step in range(4):
                n1, n2 = (T1, T2) if step < 3 else (H1, H2)
                when(-sgn(way) * step, 0, lambda p: over(ring.at[0, 0:n1, :], z1_s.at[way, step]))
                whole = (z + step) % 2 == 1
                pl.when(whole)(lambda: over(ring.at[0:NY, 0:n2, :], z2_s.at[way, step]))
                pl.when(jnp.logical_not(whole))(lambda: over(ring.at[0 : NY - 1, 0:n2, :], z2_s.at[way, step]))
            over(ring.at[0:7, 0 : T1 + H1, :], y1_s.at[way])
            when(0, 0, lambda p: y2(way, 0, p).wait_send())
            when(0, -sgn(way), lambda p: y2(way, 1, p).wait_send())

    def sgn(way):
        return 1 - 2 * way

    def z1(way, step, half, p):
        ref = ring.at[p, pl.ds(half * H1, H1), :]
        return remote(ref, ref, z1_s.at[way, step], z1_r.at[way, step, half], to_z[way])

    def y1(way, e, step, half, p):
        ref = ring.at[p, pl.ds(half * H1, H1), :]
        i = e % NZ
        return remote(ref, ref, y1_s.at[way], y1_r.at[way, i, half if step == 0 else 2], to_y[way])

    def y2(way, step, p):
        ref = ring.at[p, pl.ds(T1, T2), :] if step == 0 else ring.at[p, pl.ds(T1 + way * H2, H2), :]
        return remote(ref, ref, y2_s.at[way, step], y2_r.at[way, step], to_y[way])

    def z2(way, step, dy, p):
        ref = ring.at[p, pl.ds(T1, T2), :] if step < 3 else ring.at[p, pl.ds(T1 + way * H2, H2), :]
        return remote(ref, ref, z2_s.at[way, step], z2_r.at[way, step, dy], to_z[way])

    def y1_send(e, half):
        def f(p):
            for way in range(2):
                y1(way, e, 0, half, p).start()

        when(e, 0, f)

    def z2_send(dy):
        def f(p):
            for way in range(2):
                z2(way, 0, dy, p).start()

        when(0, dy, f)

    def take_z1(way, step, half):
        d = step + 1

        def f(p):
            z1(way, step, half, p).wait_recv()
            if d < 3 or (d == 3 and half == way):
                z1(way, d, half, p).start()

        when(-sgn(way) * d, 0, f)
        y1_send(-sgn(way) * d, half)

    def take_y1(way, e, step, half):
        def f(p):
            y1(way, e, step, half, p).wait_recv()
            if step == 0 and half == way:
                y1(way, e, 1, half, p).start()

        when(e, -sgn(way) * (step + 1), f)

    def take_y2(way, step):
        def f(p):
            y2(way, step, p).wait_recv()
            if step == 0:
                y2(way, 1, p).start()

        when(0, -sgn(way) * (step + 1), f)
        if step == 0:
            z2_send(-sgn(way) % NY)
        elif way == 1:
            z2_send(2)

    def take_z2(way, step, dy):
        d = step + 1

        def f(p):
            z2(way, step, dy, p).wait_recv()
            if d < 4:
                z2(way, d, dy, p).start()

        when(-sgn(way) * d, dy, f)

    takes = {"z1": take_z1, "y1": take_y1, "y2": take_y2, "z2": take_z2}

    def column(e, lo, hi):
        def body(i, c):
            when(e, jnp.where(i < 2, i, 5 - i), lambda p: multiply(p, 0, T1))
            return c

        lax.fori_loop(lo, hi, body, 0)

    def ring_of(d):
        def body(i, c):
            dz = d if d in (0, 4) else jnp.where(i < NY, d, -d)
            when(dz, i % NY, lambda p: multiply(p, T1, T2))
            return c

        lax.fori_loop(0, NY if d in (0, 4) else 2 * NY, body, 0)

    @pl.when(is_holder)
    def _():
        for h in range(2):
            ring[mine, pl.ds(h * HALF, HALF), :] = jnp.dot(
                onehot[pl.ds(h * HALF, HALF), :], xs[...], preferred_element_type=F32
            ).astype(BF16)
        for way in range(2):
            y2(way, 0, mine).start()
        for i in range(2):
            for way in range(2):
                z1(way, 0, i if way == 0 else 1 - i, mine).start()

    y1_send(0, 0)
    y1_send(0, 1)
    z2_send(0)
    for n, (wave, *which) in enumerate(ARRIVALS):
        takes[wave](*which)
        later = ARRIVALS[n + 1 :]
        if wave == "z2" and not any(o[0] == "z2" and o[2] == which[1] for o in later):
            ring_of(which[1] + 1)
        if wave == "y2" and not any(o[0] == "y2" for o in later):
            ring_of(0)
        if wave == "y1" and not any(o[0] == "y1" and o[2] == which[1] for o in later):
            column(which[1], 3 if which[1] == 4 else 0, 4)
        elif wave == "y1" and which[1:3] == [4, 0] and not any(o[0] == "y1" and o[2:4] == (4, 0) for o in later):
            column(4, 0, 3)

    for r in range(LIVE // 128):
        rows = pl.ds(r * 128, 128)
        gate = acc[rows, 0:FP]
        hid[rows, :] = (gate / (1.0 + jnp.exp(-gate)) * acc[rows, FP : 2 * FP]).astype(BF16)

    def slab(dy):
        yy = (y + dy) % NY
        for r in range(4):
            rows = pl.ds(r * 192, 192)
            part = jnp.dot(hid[rows, :], wd[yy], preferred_element_type=F32).astype(BF16)
            for zp in range(7):
                w[zp * NY + yy, rows, 0:OW] = part[:, zp * OW : (zp + 1) * OW]

    def part(zp, dy, r0, n):
        return w.at[zp * NY + (y + dy) % NY, pl.ds(r0, n), 0:OW]

    def add(ref, r0, n, *others):
        total = ref[pl.ds(r0, n), :].astype(F32)
        for other in others:
            total = total + other[...].astype(F32)
        return total

    zps = [(z + dz + 8) % NZ for dz in ORDER]

    def m1(k, up):
        if up:
            return remote(part(zps[k], 2, 0, H1), r1.at[0, k], s1.at[0], q1.at[0, k], up_y)
        return remote(part(zps[k], 2, H1, H1), r1.at[1, k], s1.at[1], q1.at[1, k], dn_y)

    def m2(k, up):
        if up:
            return remote(part(zps[k], 1, 0, T1), r2.at[0, k], s2.at[0], q2.at[k], up_y)
        return remote(part(zps[k], 3, 0, T1), r2.at[1, k], s2.at[1], q2.at[k], dn_y)

    def mz(k, way, dist):
        to = up_z if way == 0 else dn_z
        if dist == 4:
            rows = pl.ds(way * H1, H1)
            return remote(yz.at[k, rows, :], zr.at[way, 3, rows, :], sz.at[way, 3], qz.at[way, 3], to)
        return remote(yz.at[k], zr.at[way, dist - 1], sz.at[way, dist - 1], qz.at[way, dist - 1], to)

    def mt(k, way, dist, yp):
        to = up_z if way == 0 else dn_z
        p = zps[k] * NY + yp
        if dist == 4:
            src = w.at[p, pl.ds(T1 + way * H2, H2), 0:OW]
            dst = tz.at[way, 3, yp, pl.ds(way * H2, H2), :]
            return remote(src, dst, st.at[way, 3], qt.at[way, 3, yp], to)
        src = w.at[p, pl.ds(T1, T2), 0:OW]
        return remote(src, tz.at[way, dist - 1, yp], st.at[way, dist - 1], qt.at[way, dist - 1, yp], to)

    def my1(up):
        if up:
            return remote(part(z, 2, T1, H2), ty1.at[0], sy1.at[0], qy1.at[0], up_y)
        return remote(part(z, 2, T1 + H2, H2), ty1.at[1], sy1.at[1], qy1.at[1], dn_y)

    def my2(up):
        if up:
            return remote(part(z, 1, T1, T2), ty2.at[0], sy2.at[0], qy2.at[0], up_y)
        return remote(part(z, 3, T1, T2), ty2.at[1], sy2.at[1], qy2.at[1], dn_y)

    def guarded(k, f):
        pl.when(zps[k] < 7)(f)

    def second(k):
        def f():
            for way in range(2):
                m1(k, way == 0).wait_recv()
                ref = part(zps[k], 1 if way == 0 else 3, way * H1, H1)
                ref[...] = (ref[...].astype(F32) + r1[way, k].astype(F32)).astype(BF16)
                m2(k, way == 0).start()

        guarded(k, f)

    def line(k):
        dz = ORDER[k]

        def f():
            both = r2.at[:, k]
            pltpu.make_async_copy(both, both, q2.at[k]).wait()
            ways = {4: (), 0: (0, 1)}.get(dz, (0,) if dz > 0 else (1,))
            for way in ways:
                mz(k, way, abs(dz) + 1).wait_recv()
            for h in range(2):
                rows = pl.ds(h * H1, H1)
                total = part(zps[k], 0, h * H1, H1)[...].astype(F32)
                total = total + r2[0, k, rows, :].astype(F32) + r2[1, k, rows, :].astype(F32)
                for way in ways:
                    if abs(dz) < 3 or way == h:
                        total = total + zr[way, abs(dz), rows, :].astype(F32)
                if dz == 0:
                    res[rows, :] = total.astype(BF16)
                else:
                    yz[k, rows, :] = total.astype(BF16)
            if dz == 4:
                mz(k, 0, 4).start()
                mz(k, 1, 4).start()
            elif dz != 0:
                mz(k, ways[0], abs(dz)).start()

        guarded(k, f)

    def plane(dist):
        if dist == 4:

            def f():
                for yp in range(NY):
                    mt(0, 0, 4, yp).start()
                    mt(0, 1, 4, yp).start()

            guarded(0, f)
            return
        if dist == 0:
            k = len(ORDER) - 1

            def f():
                for dy in (2, 1, 3, 0):
                    yp = (y + dy) % NY
                    mt(k, 0, 1, yp).wait_recv()
                    mt(k, 1, 1, yp).wait_recv()
                    ref = part(z, dy, T1, T2)
                    ref[...] = (ref[...].astype(F32) + tz[0, 0, yp].astype(F32) + tz[1, 0, yp].astype(F32)).astype(BF16)
                    if dy == 2:
                        my1(True).start()
                        my1(False).start()

            guarded(k, f)
            return
        for yp in range(NY):
            for way in range(2):
                k = ORDER.index(dist if way == 0 else -dist)

                def f(k=k, way=way, yp=yp):
                    mt(k, way, dist + 1, yp).wait_recv()
                    if dist == 3:
                        ref = w.at[zps[k] * NY + yp, pl.ds(T1 + way * H2, H2), 0:OW]
                        got = tz[way, 3, yp, pl.ds(way * H2, H2), :]
                    else:
                        ref = w.at[zps[k] * NY + yp, pl.ds(T1, T2), 0:OW]
                        got = tz[way, dist, yp]
                    ref[...] = (ref[...].astype(F32) + got.astype(F32)).astype(BF16)
                    mt(k, way, dist, yp).start()

                guarded(k, f)

    def cross():
        def f():
            for way in range(2):
                my1(way == 0).wait_recv()
                ref = part(z, 1 if way == 0 else 3, T1 + way * H2, H2)
                ref[...] = (ref[...].astype(F32) + ty1[way].astype(F32)).astype(BF16)
                my2(way == 0).start()

        pl.when(z < 7)(f)

    slab(2)
    for k in range(8):

        def f(k=k):
            m1(k, True).start()
            m1(k, False).start()

        guarded(k, f)
    slab(1)
    slab(3)
    slab(0)
    plane(4)
    second(0)
    second(1)
    plane(3)
    for k in range(2, 8):
        second(k)
    plane(2)
    line(0)
    plane(1)
    line(1)
    line(2)
    line(3)
    plane(0)
    line(4)
    cross()

    jrow = lax.broadcasted_iota(I32, (OROW, LIVE), 0)
    diff = lax.broadcasted_iota(I32, (OROW, LIVE), 1) - jrow
    for i in range(N):
        hit = (diff == offs[i]) & (jrow < counts[i])
        back[i * OROW : (i + 1) * OROW, :] = jnp.where(hit, 1.0, 0.0).astype(BF16)

    gathered()
    line(5)
    line(6)
    line(7)

    @pl.when(z < 7)
    def _():
        my2(True).wait_recv()
        my2(False).wait_recv()
        total = part(z, 0, T1, T2)[...].astype(F32) + ty2[0].astype(F32) + ty2[1].astype(F32)
        res[T1:, :] = total.astype(BF16)
        for h in range(4):
            slots = jnp.dot(back[h * 384 : (h + 1) * 384, :], res[...], preferred_element_type=F32).astype(BF16)
            for i in range(8):
                osrc[8 * h + i] = slots[i * OROW : (i + 1) * OROW]
        odst[g] = osrc[g]

        def give(i, c):
            to = (g + i) % N
            remote(osrc.at[to], odst.at[g], o_s, o_r, to).start()
            return c

        lax.fori_loop(1, N, give, 0)

    for way in range(2):
        over(r1.at[way, 0:7], s1.at[way])
        over(r2.at[way, 0:7], s2.at[way])
        for k, dz in enumerate(ORDER):
            if dz == 4 or (dz > 0 and way == 0) or (dz < 0 and way == 1):

                def f(k=k, way=way, dist=abs(dz)):
                    mz(k, way, dist).wait_send()
                    over(tz.at[way, 0, :, 0 : H2 if dist == 4 else T2, :], st.at[way, dist - 1])

                guarded(k, f)

    @pl.when(is_holder)
    def _():
        some = asrc.at[pl.ds(0, HOLD - 1)]
        pltpu.make_async_copy(some, some, a_s).wait()

    @pl.when(jnp.logical_not(is_holder))
    def _():
        some = asrc.at[pl.ds(0, HOLD)]
        pltpu.make_async_copy(some, some, a_s).wait()

    @pl.when(z < 7)
    def _():
        for way in range(2):
            my1(way == 0).wait_send()
            my2(way == 0).wait_send()
        some = odst.at[pl.ds(0, HOLD - 1)]
        pltpu.make_async_copy(some, some, o_r).wait()
        some = osrc.at[pl.ds(0, N - 1)]
        pltpu.make_async_copy(some, some, o_s).wait()

    @pl.when(z == 7)
    def _():
        some = odst.at[pl.ds(0, HOLD)]
        pltpu.make_async_copy(some, some, o_r).wait()

    for p in range(HOLD):
        out[:, p * OW : (p + 1) * OW] = odst[p][:CAP]


def shards(tv, ts, counts, gv, gs, uv, us, dv, ds):
    any_space = pl.BlockSpec(memory_space=pl.ANY)
    vmem, dma = pltpu.VMEM, pltpu.SemaphoreType.DMA
    return pl.pallas_call(
        kernel,
        out_shape=jax.ShapeDtypeStruct((CAP, DO), BF16),
        in_specs=[pl.BlockSpec(memory_space=pltpu.SMEM)] + [any_space] * 8,
        out_specs=pl.BlockSpec(memory_space=pltpu.VMEM),
        scratch_shapes=[
            vmem((CAP, D), BF16),
            vmem((CAP, D // 128), BF16),
            vmem((FF, D), BF16),
            vmem((FF, D // 128), F32),
            vmem((D // 128, FF), F32),
            vmem((FF, D), BF16),
            vmem((FF, D // 128), F32),
            vmem((D // 128, FF), F32),
            vmem((FF, DO), BF16),
            vmem((FF, DO // 128), F32),
            vmem((DO // 128, FF), F32),
            vmem((HOLD, 2 * CAP, 128), BF16),
            vmem((N, 2 * CAP, 128), BF16),
            vmem((N * CAP, PW), BF16),
            vmem((LIVE, N * CAP), BF16),
            vmem((N * OROW, LIVE), BF16),
            vmem((HOLD, 2 * FP, PW), BF16),
            vmem((NY, FP, DO // NY), BF16),
            vmem((LIVE, 2 * FP), F32),
            vmem((LIVE, FP), BF16),
            vmem((HOLD, LIVE, PW), BF16),
            vmem((2, 8, H1, OW), BF16),
            vmem((2, 8, T1, OW), BF16),
            vmem((8, T1, OW), BF16),
            vmem((2, 4, T1, OW), BF16),
            vmem((2, 4, NY, T2, OW), BF16),
            vmem((2, H2, OW), BF16),
            vmem((2, T2, OW), BF16),
            vmem((LIVE, OW), BF16),
            vmem((N, OROW, OW), BF16),
            vmem((HOLD, OROW, OW), BF16),
            dma((8,)),
            dma,
            dma,
            dma((2, 4)),
            dma((2, 4, 2)),
            dma((2,)),
            dma((2, NZ, 3)),
            dma((2, 2)),
            dma((2, 2)),
            dma((2, 4)),
            dma((2, 4, NY)),
            dma((2,)),
            dma((2, 8)),
            dma((2,)),
            dma((8,)),
            dma((2, 4)),
            dma((2, 4)),
            dma((2, 4)),
            dma((2, 4, NY)),
            dma((2,)),
            dma((2,)),
            dma((2,)),
            dma((2,)),
            dma,
            dma,
        ],
        compiler_params=pltpu.CompilerParams(
            collective_id=0, has_side_effects=True, vmem_limit_bytes=60 * 2**20
        ),
        cost_estimate=pl.CostEstimate(flops=10**10, bytes_accessed=12 * 10**6, transcendentals=LIVE * FF),
        name="swiglu",
    )(counts, tv, ts, gv, gs.T, uv, us.T, dv, ds.T)


def solution(mesh):
    rows, split = P(("replica", "group"), None), P("group", None)
    in_specs = (rows, rows, P("replica")) + (split,) * 6
    return jax.shard_map(shards, mesh=mesh, in_specs=in_specs, out_specs=rows, check_vma=False)
```

```python
import jax
import jax.numpy as jnp
from jax import lax
from jax.experimental import pallas as pl
from jax.experimental.pallas import tpu as pltpu
from jax.sharding import PartitionSpec as P

F32, BF16, I32 = jnp.float32, jnp.bfloat16, jnp.int32
N, NZ, NY = 32, 8, 4
CAP, LIVE = 40, 768
D, DO, FF = 7168, 3584, 288
HOLD = 28
PW, OW = 256, 128
HALF = LIVE // 2
FP = 384
T1 = 448
T2 = LIVE - T1
H1, H2 = T1 // 2, T2 // 2
S1 = 448
S2 = LIVE - S1
K1, K2 = S1 // 2, S2 // 2
HELD = tuple(d for d in range(N) if d % 9)
OROW = 48
ORDER = (4, 3, -3, 2, -2, 1, -1, 0)

ARRIVALS = (
    ("z1", 1, 0, 1), ("z1", 0, 0, 0), ("y2", 1, 0), ("z1", 0, 0, 1), ("y2", 0, 0), ("z1", 0, 1, 0), ("z1", 1, 1, 1),
    ("y1", 0, -1, 0, 0), ("y1", 1, 0, 0, 0), ("y1", 0, 0, 0, 1), ("z1", 1, 0, 0), ("y1", 1, -1, 0, 1),
    ("y1", 1, -1, 0, 0), ("y2", 0, 1), ("y2", 1, 1), ("z1", 0, 1, 1), ("z1", 1, 2, 1), ("y1", 1, 2, 0, 1),
    ("z2", 0, 0, 1), ("y1", 1, 1, 0, 1), ("z2", 1, 0, 0), ("z1", 1, 1, 0), ("y1", 0, 1, 0, 1), ("z2", 0, 0, 3),
    ("y1", 0, 0, 0, 0), ("z2", 1, 0, 3), ("z1", 1, 3, 1), ("z2", 0, 0, 0), ("z2", 1, 0, 2), ("y1", 0, -2, 0, 1),
    ("y1", 1, 0, 0, 1), ("z2", 0, 0, 2), ("z1", 0, 2, 1), ("y1", 0, -1, 1, 0), ("z1", 0, 2, 0), ("y1", 0, 1, 0, 0),
    ("z2", 1, 0, 1), ("z1", 1, 2, 0), ("z2", 0, 1, 1), ("z2", 1, 1, 0), ("z2", 1, 1, 2), ("z2", 0, 1, 0),
    ("y1", 0, 2, 0, 0), ("y1", 0, 4, 0, 1), ("z2", 0, 1, 3), ("y1", 1, -2, 0, 1), ("y1", 1, 2, 0, 0),
    ("y1", 0, -2, 0, 0), ("y1", 0, -1, 0, 1), ("z2", 1, 1, 1), ("y1", 0, 3, 0, 1), ("y1", 1, -1, 1, 1),
    ("y1", 1, 2, 1, 1), ("z2", 1, 1, 3), ("z2", 0, 1, 2), ("z1", 0, 3, 0), ("y1", 1, -3, 0, 1), ("z2", 0, 2, 1),
    ("y1", 1, -2, 0, 0), ("y1", 1, 0, 1, 1), ("y1", 0, 3, 0, 0), ("y1", 0, 0, 1, 0), ("y1", 0, 2, 1, 0),
    ("y1", 1, 3, 0, 0), ("y1", 1, 3, 0, 1), ("y1", 1, 4, 0, 1), ("y1", 1, -2, 1, 1), ("z2", 1, 2, 0),
    ("y1", 0, 2, 0, 1), ("y1", 1, -3, 0, 0), ("z2", 0, 2, 0), ("y1", 0, -3, 0, 0), ("y1", 0, -2, 1, 0),
    ("z2", 1, 2, 1), ("y1", 1, 1, 0, 0), ("y1", 0, 1, 1, 0), ("y1", 0, 4, 0, 0), ("z2", 0, 2, 3), ("z2", 1, 2, 2),
    ("y1", 1, 1, 1, 1), ("y1", 0, 3, 1, 0), ("z2", 0, 2, 2), ("z2", 1, 2, 3), ("z2", 0, 3, 1), ("y1", 1, 3, 1, 1),
    ("y1", 1, 4, 0, 0), ("z2", 0, 3, 0), ("y1", 0, -3, 0, 1), ("z2", 1, 3, 0), ("y1", 1, 4, 1, 1),
    ("y1", 0, -3, 1, 0), ("z2", 1, 3, 1), ("y1", 1, -3, 1, 1), ("y1", 0, 4, 1, 0), ("z2", 0, 3, 3), ("z2", 0, 3, 2),
    ("z2", 1, 3, 2), ("z2", 1, 3, 3),
)

SUMS = (
    ("tz", 0, 3, 1), ("tz", 1, 3, 0), ("ya", 1, 4), ("tz", 0, 3, 0), ("tz", 0, 3, 3), ("tz", 1, 3, 1),
    ("tz", 1, 3, 2), ("tz", 0, 3, 2), ("ya", 1, -3), ("ya", 0, 4), ("ya", 1, 3), ("tz", 0, 2, 1), ("ya", 0, -3),
    ("tz", 1, 3, 3), ("tz", 0, 2, 0), ("ya", 0, 3), ("ya", 0, -2), ("tz", 1, 2, 0), ("tz", 0, 2, 3), ("ya", 1, -2),
    ("tz", 1, 2, 2), ("ya", 0, 2), ("line", 4), ("tz", 0, 2, 2), ("tz", 1, 2, 1), ("ya", 1, 2), ("ya", 0, 1),
    ("tz", 0, 1, 0), ("ya", 1, -1), ("tz", 1, 2, 3), ("line", -3), ("line", 3), ("tz", 1, 1, 2), ("tz", 0, 1, 2),
    ("ya", 0, 0), ("ya", 1, 0), ("ya", 0, -1), ("tz", 0, 1, 3), ("tz", 1, 1, 3), ("ya", 1, 1), ("line", -2),
    ("line", 2), ("tz", 1, 1, 1), ("tz", 0, 1, 1), ("tz0", 3), ("tz", 1, 1, 0), ("tz0", 2), ("line", -1), ("line", 1),
    ("tz0", 1), ("tz0", 0), ("line", 0), ("fin",),
)


def kernel(
    counts, tv_h, ts_h, gv_h, gs_h, uv_h, us_h, dv_h, ds_h, out,
    tv, ts, gv, gs, gst, uv, us, ust, dv, ds, dst, asrc, adst, xs, onehot, back, w, wd, acc, hid, ring,
    r1, r2, yz, zr, tz, ty, far, res, osrc, odst,
    ld, a_s, a_r, z1_s, z1_r, y1_s, y1_r, y2_s, y2_r, z2_s, z2_r, s1, q1, s2, q2, sz, qz, st, qt, sy, qy, o_s, o_r,
):
    rep = lax.axis_index("replica")
    g = lax.axis_index("group")
    z, y = g // NY, g % NY
    up_y, dn_y = z * NY + (y + 1) % NY, z * NY + (y + 3) % NY
    up_z, dn_z = ((z + 1) % NZ) * NY + y, ((z + 7) % NZ) * NY + y
    def holds(dev):
        return dev % 9 != 0

    def piece_of(dev):
        return jnp.maximum(dev - 1 - dev // 9, 0)

    is_holder = holds(g)
    mine = piece_of(g)

    def remote(src, dst, send, recv, to):
        return pltpu.make_async_remote_copy(
            src, dst, send, recv, device_id=(rep, to), device_id_type=pl.DeviceIdType.MESH
        )

    loads = [
        pltpu.make_async_copy(a, b, ld.at[i])
        for i, (a, b) in enumerate(
            ((tv_h, tv), (ts_h, ts), (gv_h, gv), (gs_h, gst), (uv_h, uv), (us_h, ust), (dv_h, dv), (ds_h, dst))
        )
    ]
    for load in loads:
        load.start()
    barrier = pltpu.get_barrier_semaphore()

    def greet(i, c):
        pl.semaphore_signal(barrier, inc=1, device_id=(rep, (g + i) % N), device_id_type=pl.DeviceIdType.MESH)
        return c

    lax.fori_loop(1, N, greet, 0)

    loads[0].wait()
    loads[1].wait()
    tsf = ts[...].astype(F32)
    for p in range(HOLD):
        lo = tv[:, PW * p : PW * p + 128].astype(F32) * tsf[:, 2 * p : 2 * p + 1]
        hi = tv[:, PW * p + 128 : PW * p + 256].astype(F32) * tsf[:, 2 * p + 1 : 2 * p + 2]
        asrc[p] = jnp.concatenate([lo, hi], axis=0).astype(BF16)
    pl.semaphore_wait(barrier, N - 1)

    def far_first(i):
        k = i // NY
        dz = 4 + (k + 1) // 2 * (1 - 2 * (k % 2))
        return ((z + dz) % NZ) * NY + (y + i) % NY

    def scatter(i, c):
        to = far_first(i)

        @pl.when(holds(to) & (to != g))
        def _():
            remote(asrc.at[piece_of(to)], adst.at[g], a_s, a_r, to).start()

        return c

    lax.fori_loop(0, N, scatter, 0)

    offs, off = [], jnp.int32(0)
    lane = lax.broadcasted_iota(I32, (16, N * CAP), 1)
    target = jnp.full((16, N * CAP), -1, I32)
    for i in range(N):
        c = counts[i]
        rel = lane - CAP * i
        target = jnp.where((rel >= 0) & (rel < c), rel + off, target)
        offs.append(off)
        off = off + c
    row16 = lax.broadcasted_iota(I32, (16, N * CAP), 0)

    def build(r, c):
        hit = target == row16 + r * 16
        onehot[pl.ds(pl.multiple_of(r * 16, 16), 16), :] = jnp.where(hit, 1.0, 0.0).astype(BF16)
        return c

    lax.fori_loop(0, LIVE // 16, build, 0)

    for v, s, st_, at in ((gv, gs, gst, 0), (uv, us, ust, FP)):
        loads[2 if at == 0 else 4].wait()
        loads[3 if at == 0 else 5].wait()
        s[...] = st_[...].T

        def deq(r, c, v=v, s=s, at=at):
            r0 = pl.multiple_of(r * 32, 32)
            sf = s[pl.ds(r0, 32), :]
            for b in range(D // 128):
                val = v[pl.ds(r0, 32), 128 * b : 128 * b + 128].astype(F32) * sf[:, b : b + 1]
                w[b // 2, pl.ds(at + r0, 32), 128 * (b % 2) : 128 * (b % 2) + 128] = val.astype(BF16)
            return c

        lax.fori_loop(0, FF // 32, deq, 0)

    loads[6].wait()
    loads[7].wait()
    ds[...] = dst[...].T

    def deq_down(r, c):
        r0 = pl.multiple_of(r * 32, 32)
        sf = ds[pl.ds(r0, 32), :]
        for b in range(HOLD):
            val = dv[pl.ds(r0, 32), 128 * b : 128 * b + 128].astype(F32) * sf[:, b : b + 1]
            zz, yy = HELD[b] // NY, HELD[b] % NY
            i = zz - int(zz > 2 * yy)
            wd[yy, pl.ds(r0, 32), 128 * i : 128 * i + 128] = val.astype(BF16)
        return c

    lax.fori_loop(0, FF // 32, deq_down, 0)
    wd[:, FF:, :] = jnp.zeros((NY, FP - FF, DO // NY), BF16)

    def pad(p, c):
        w[p, FF:FP, :] = jnp.zeros((FP - FF, PW), BF16)
        w[p, FP + FF :, :] = jnp.zeros((FP - FF, PW), BF16)
        return c

    lax.fori_loop(0, HOLD, pad, 0)
    acc[...] = jnp.zeros_like(acc)

    jrow = lax.broadcasted_iota(I32, (OROW, LIVE), 0)
    diff = lax.broadcasted_iota(I32, (OROW, LIVE), 1) - jrow
    for i in range(N):
        hit = (diff == offs[i]) & (jrow < counts[i])
        back[i * OROW : (i + 1) * OROW, :] = jnp.where(hit, 1.0, 0.0).astype(BF16)

    @pl.when(is_holder)
    def _():
        adst[g] = asrc[mine]
        pltpu.make_async_copy(adst.at[pl.ds(0, N - 1)], adst.at[pl.ds(0, N - 1)], a_r).wait()

        def spread(k, c):
            a = adst[2 * k].astype(F32)
            b = adst[2 * k + 1].astype(F32)
            rows = pl.ds(pl.multiple_of(k * 80, 16), 80)
            xs[rows, 0:128] = jnp.concatenate([a[:CAP], b[:CAP]], axis=0).astype(BF16)
            xs[rows, 128:256] = jnp.concatenate([a[CAP:], b[CAP:]], axis=0).astype(BF16)
            return c

        lax.fori_loop(0, N // 2, spread, 0)

    def multiply(src, r0, n):
        acc[r0 : r0 + n, :] += lax.dot_general(
            ring[src, r0 : r0 + n, :], w[src], (((1,), (1,)), ((), ())), preferred_element_type=F32
        )

    def at(dz, dy):
        dev = ((z + dz + 8) % NZ) * NY + (y + dy + 4) % NY
        return holds(dev), piece_of(dev)

    def when(dz, dy, f):
        live, p = at(dz, dy)
        pl.when(live)(lambda: f(p))

    to_z, to_y = (up_z, dn_z), (up_y, dn_y)

    def over(ref, sem):
        pltpu.make_async_copy(ref, ref, sem).wait()

    def gathered():
        for way in range(2):
            for step in range(4):
                n1, n2 = (T1, T2) if step < 3 else (H1, H2)
                when(-sgn(way) * step, 0, lambda p: over(ring.at[0, 0:n1, :], z1_s.at[way, step]))
                whole = (z + step) % 2 == 1
                pl.when(whole)(lambda: over(ring.at[0:NY, 0:n2, :], z2_s.at[way, step]))
                pl.when(jnp.logical_not(whole))(lambda: over(ring.at[0 : NY - 1, 0:n2, :], z2_s.at[way, step]))
            over(ring.at[0:7, 0 : T1 + H1, :], y1_s.at[way])
            when(0, 0, lambda p: y2(way, 0, p).wait_send())
            when(0, -sgn(way), lambda p: y2(way, 1, p).wait_send())

    def sgn(way):
        return 1 - 2 * way

    def z1(way, step, half, p):
        ref = ring.at[p, pl.ds(half * H1, H1), :]
        return remote(ref, ref, z1_s.at[way, step], z1_r.at[way, step, half], to_z[way])

    def y1(way, e, step, half, p):
        ref = ring.at[p, pl.ds(half * H1, H1), :]
        i = e % NZ
        return remote(ref, ref, y1_s.at[way], y1_r.at[way, i, half if step == 0 else 2], to_y[way])

    def y2(way, step, p):
        ref = ring.at[p, pl.ds(T1, T2), :] if step == 0 else ring.at[p, pl.ds(T1 + way * H2, H2), :]
        return remote(ref, ref, y2_s.at[way, step], y2_r.at[way, step], to_y[way])

    def z2(way, step, dy, p):
        ref = ring.at[p, pl.ds(T1, T2), :] if step < 3 else ring.at[p, pl.ds(T1 + way * H2, H2), :]
        return remote(ref, ref, z2_s.at[way, step], z2_r.at[way, step, dy], to_z[way])

    def y1_send(e, half):
        def f(p):
            for way in range(2):
                y1(way, e, 0, half, p).start()

        when(e, 0, f)

    def z2_send(dy):
        def f(p):
            for way in range(2):
                z2(way, 0, dy, p).start()

        when(0, dy, f)

    def take_z1(way, step, half):
        d = step + 1

        def f(p):
            z1(way, step, half, p).wait_recv()
            if d < 3 or (d == 3 and half == way):
                z1(way, d, half, p).start()

        when(-sgn(way) * d, 0, f)
        y1_send(-sgn(way) * d, half)

    def take_y1(way, e, step, half):
        def f(p):
            y1(way, e, step, half, p).wait_recv()
            if step == 0 and half == way:
                y1(way, e, 1, half, p).start()

        when(e, -sgn(way) * (step + 1), f)

    def take_y2(way, step):
        def f(p):
            y2(way, step, p).wait_recv()
            if step == 0:
                y2(way, 1, p).start()

        when(0, -sgn(way) * (step + 1), f)
        if step == 0:
            z2_send(-sgn(way) % NY)
        elif way == 1:
            z2_send(2)

    def take_z2(way, step, dy):
        d = step + 1

        def f(p):
            z2(way, step, dy, p).wait_recv()
            if d < 4:
                z2(way, d, dy, p).start()

        when(-sgn(way) * d, dy, f)

    takes = {"z1": take_z1, "y1": take_y1, "y2": take_y2, "z2": take_z2}

    def column(e, lo, hi):
        def body(i, c):
            when(e, jnp.where(i < 2, i, 5 - i), lambda p: multiply(p, 0, T1))
            return c

        lax.fori_loop(lo, hi, body, 0)

    def ring_of(d):
        def body(i, c):
            dz = d if d in (0, 4) else jnp.where(i < NY, d, -d)
            when(dz, i % NY, lambda p: multiply(p, T1, T2))
            return c

        lax.fori_loop(0, NY if d in (0, 4) else 2 * NY, body, 0)

    @pl.when(is_holder)
    def _():
        for h in range(2):
            ring[mine, pl.ds(h * HALF, HALF), :] = jnp.dot(
                onehot[pl.ds(h * HALF, HALF), :], xs[...], preferred_element_type=F32
            ).astype(BF16)
        for way in range(2):
            y2(way, 0, mine).start()
        for i in range(2):
            for way in range(2):
                z1(way, 0, i if way == 0 else 1 - i, mine).start()

    y1_send(0, 0)
    y1_send(0, 1)
    z2_send(0)
    for n, (wave, *which) in enumerate(ARRIVALS):
        takes[wave](*which)
        later = ARRIVALS[n + 1 :]
        if wave == "z2" and not any(o[0] == "z2" and o[2] == which[1] for o in later):
            ring_of(which[1] + 1)
        if wave == "y2" and not any(o[0] == "y2" for o in later):
            ring_of(0)
        if wave == "y1" and not any(o[0] == "y1" and o[2] == which[1] for o in later):
            column(which[1], 3 if which[1] == 4 else 0, 4)
        if wave == "y1" and which[1:3] == [4, 0] and not any(o[0] == "y1" and o[2:4] == (4, 0) for o in later):
            column(4, 0, 3)

    for r in range(LIVE // 128):
        rows = pl.ds(r * 128, 128)
        gate = acc[rows, 0:FP]
        hid[rows, :] = (gate / (1.0 + jnp.exp(-gate)) * acc[rows, FP : 2 * FP]).astype(BF16)

    def slab(dy):
        yy = (y + dy) % NY
        for r in range(4):
            rows = pl.ds(r * 192, 192)
            got = jnp.dot(hid[rows, :], wd[yy], preferred_element_type=F32).astype(BF16)
            for i in range(7):
                zz = i + (i >= 2 * yy).astype(I32)
                w[piece_of(zz * NY + yy), rows, 0:OW] = got[:, i * OW : (i + 1) * OW]

    def slab_far(dy):
        yy, zz = (y + dy) % NY, (z + 4) % NZ
        i = zz - (zz > 2 * yy).astype(I32)
        cols = wd[yy, :, pl.ds(pl.multiple_of(i * OW, OW), OW)]
        far[dy] = jnp.dot(hid[S1:, :], cols, preferred_element_type=F32).astype(BF16)

    def part(p, r0, n):
        return w.at[p, r0 : r0 + n, 0:OW]

    def m1(way, e, p):
        return remote(part(p, way * K1, K1), r1.at[way, e % NZ], s1.at[way], q1.at[way, e % NZ], to_y[way])

    def m2(way, e, p):
        return remote(part(p, 0, S1), r2.at[way, e % NZ], s2.at[way], q2.at[e % NZ], to_y[way])

    def mz(way, dist):
        e = sgn(way) * dist % NZ
        if dist == 4:
            rows = pl.ds(way * K1, K1)
            return remote(yz.at[e, rows, :], zr.at[way, 3, rows, :], sz.at[way, 3], qz.at[way, 3], to_z[way])
        return remote(yz.at[e], zr.at[way, dist - 1], sz.at[way, dist - 1], qz.at[way, dist - 1], to_z[way])

    def mt(way, dist, dy, p):
        if dist == 4:
            rows = pl.ds(way * K2, K2)
            src, dst = far.at[dy, rows, :], tz.at[way, 3, dy, rows, :]
        else:
            src, dst = part(p, S1, S2), tz.at[way, dist - 1, dy]
        return remote(src, dst, st.at[way, dist - 1], qt.at[way, dist - 1, dy], to_z[way])

    def my(dy, p):
        to = z * NY + (y + dy) % NY
        return remote(part(p, S1, S2), ty.at[dy - 1], sy.at[dy - 1], qy.at[dy - 1], to)

    def add(ref, *others):
        total = ref[...].astype(F32)
        for other in others:
            total = total + other.astype(F32)
        return total

    def sum_ya(way, e):
        def f(p):
            m1(way, e, p).wait_recv()
            ref = part(p, way * K1, K1)
            ref[...] = add(ref, r1[way, e % NZ]).astype(BF16)
            m2(way, e, p).start()

        when(e, sgn(way), f)

    def sum_line(e):
        ways = {4: (), 0: (0, 1)}.get(e, (0,) if e > 0 else (1,))

        def f(p):
            over(r2.at[:, e % NZ], q2.at[e % NZ])
            for way in ways:
                mz(way, abs(e) + 1).wait_recv()
            for h in range(2):
                rows = pl.ds(h * K1, K1)
                more = [zr[way, abs(e), rows, :] for way in ways if abs(e) < 3 or way == h]
                total = add(part(p, h * K1, K1), r2[0, e % NZ, rows, :], r2[1, e % NZ, rows, :], *more)
                if e == 0:
                    res[rows, :] = total.astype(BF16)
                else:
                    yz[e % NZ, rows, :] = total.astype(BF16)
            if e == 4:
                mz(0, 4).start()
                mz(1, 4).start()
            elif e != 0:
                mz(ways[0], abs(e)).start()

        when(e, 0, f)

    def sum_tz(way, d, dy):
        def f(p):
            mt(way, d + 1, dy, p).wait_recv()
            if d == 3:
                ref, got = part(p, S1 + way * K2, K2), tz[way, 3, dy, pl.ds(way * K2, K2), :]
            else:
                ref, got = part(p, S1, S2), tz[way, d, dy]
            ref[...] = add(ref, got).astype(BF16)
            mt(way, d, dy, p).start()

        when(sgn(way) * d, dy, f)

    def sum_tz0(dy):
        def f(p):
            for way in range(2):
                mt(way, 1, dy, p).wait_recv()
            ref = part(p, S1, S2)
            ref[...] = add(ref, tz[0, 0, dy], tz[1, 0, dy]).astype(BF16)
            if dy:
                my(dy, p).start()

        when(0, dy, f)

    def sum_fin():
        def f(p):
            for dy in range(1, NY):
                my(dy, p).wait_recv()
            res[S1:, :] = add(part(p, S1, S2), ty[0], ty[1], ty[2]).astype(BF16)

        when(0, 0, f)

    sums = {"ya": sum_ya, "line": sum_line, "tz": sum_tz, "tz0": sum_tz0, "fin": sum_fin}
    for dy in range(NY):
        slab_far(dy)
    for dy in range(NY):

        def f(p, dy=dy):
            mt(0, 4, dy, p).start()
            mt(1, 4, dy, p).start()

        when(4, dy, f)
    slab(2)
    for e in ORDER:

        def f(p, e=e):
            m1(0, e, p).start()
            m1(1, e, p).start()

        when(e, 2, f)
    slab(1)
    slab(3)
    slab(0)
    for n, (wave, *which) in enumerate(SUMS):
        if n == len(SUMS) // 2:
            gathered()
        sums[wave](*which)

    @pl.when(is_holder)
    def _():
        for h in range(4):
            slots = jnp.dot(back[h * 384 : (h + 1) * 384, :], res[...], preferred_element_type=F32).astype(BF16)
            for i in range(8):
                osrc[8 * h + i] = slots[i * OROW : (i + 1) * OROW]
        odst[mine] = osrc[g]

        def give(i, c):
            to = far_first(i)

            @pl.when(to != g)
            def _():
                remote(osrc.at[to], odst.at[mine], o_s, o_r, to).start()

            return c

        lax.fori_loop(0, N, give, 0)

    for way in range(2):
        over(r1.at[way, 0:7], s1.at[way])
        over(r2.at[way, 0:7], s2.at[way])
        for dist in range(1, 5):
            when(sgn(way) * dist, 0, lambda p: mz(way, dist).wait_send())
            n2 = S2 if dist < 4 else K2
            whole = (z + dist) % 2 == 1
            pl.when(whole)(lambda: over(tz.at[way, 0, :, 0:n2, :], st.at[way, dist - 1]))
            pl.when(jnp.logical_not(whole))(lambda: over(tz.at[way, 0, 0 : NY - 1, 0:n2, :], st.at[way, dist - 1]))

    for dy in range(1, NY):
        when(0, dy, lambda p: my(dy, p).wait_send())

    @pl.when(is_holder)
    def _():
        over(asrc.at[0 : HOLD - 1], a_s)
        over(odst.at[0 : HOLD - 1], o_r)
        over(osrc.at[0 : N - 1], o_s)

    @pl.when(jnp.logical_not(is_holder))
    def _():
        over(asrc.at[0:HOLD], a_s)
        over(odst.at[0:HOLD], o_r)

    for p in range(HOLD):
        out[:, p * OW : (p + 1) * OW] = odst[p][:CAP]


def shards(tv, ts, counts, gv, gs, uv, us, dv, ds):
    any_space = pl.BlockSpec(memory_space=pl.ANY)
    vmem, dma = pltpu.VMEM, pltpu.SemaphoreType.DMA
    return pl.pallas_call(
        kernel,
        out_shape=jax.ShapeDtypeStruct((CAP, DO), BF16),
        in_specs=[pl.BlockSpec(memory_space=pltpu.SMEM)] + [any_space] * 8,
        out_specs=pl.BlockSpec(memory_space=pltpu.VMEM),
        scratch_shapes=[
            vmem((CAP, D), BF16),
            vmem((CAP, D // 128), BF16),
            vmem((FF, D), BF16),
            vmem((FF, D // 128), F32),
            vmem((D // 128, FF), F32),
            vmem((FF, D), BF16),
            vmem((FF, D // 128), F32),
            vmem((D // 128, FF), F32),
            vmem((FF, DO), BF16),
            vmem((FF, DO // 128), F32),
            vmem((DO // 128, FF), F32),
            vmem((HOLD, 2 * CAP, 128), BF16),
            vmem((N, 2 * CAP, 128), BF16),
            vmem((N * CAP, PW), BF16),
            vmem((LIVE, N * CAP), BF16),
            vmem((N * OROW, LIVE), BF16),
            vmem((HOLD, 2 * FP, PW), BF16),
            vmem((NY, FP, DO // NY), BF16),
            vmem((LIVE, 2 * FP), F32),
            vmem((LIVE, FP), BF16),
            vmem((HOLD, LIVE, PW), BF16),
            vmem((2, 8, K1, OW), BF16),
            vmem((2, 8, S1, OW), BF16),
            vmem((8, S1, OW), BF16),
            vmem((2, 4, S1, OW), BF16),
            vmem((2, 4, NY, S2, OW), BF16),
            vmem((3, S2, OW), BF16),
            vmem((NY, S2, OW), BF16),
            vmem((LIVE, OW), BF16),
            vmem((N, OROW, OW), BF16),
            vmem((HOLD, OROW, OW), BF16),
            dma((8,)),
            dma,
            dma,
            dma((2, 4)),
            dma((2, 4, 2)),
            dma((2,)),
            dma((2, NZ, 3)),
            dma((2, 2)),
            dma((2, 2)),
            dma((2, 4)),
            dma((2, 4, NY)),
            dma((2,)),
            dma((2, 8)),
            dma((2,)),
            dma((8,)),
            dma((2, 4)),
            dma((2, 4)),
            dma((2, 4)),
            dma((2, 4, NY)),
            dma((3,)),
            dma((3,)),
            dma,
            dma,
        ],
        compiler_params=pltpu.CompilerParams(
            collective_id=0, has_side_effects=True, vmem_limit_bytes=60 * 2**20
        ),
        cost_estimate=pl.CostEstimate(flops=10**10, bytes_accessed=12 * 10**6, transcendentals=LIVE * FF),
        name="swiglu",
    )(counts, tv, ts, gv, gs.T, uv, us.T, dv, ds.T)


def solution(mesh):
    rows, split = P(("replica", "group"), None), P("group", None)
    in_specs = (rows, rows, P("replica")) + (split,) * 6
    return jax.shard_map(shards, mesh=mesh, in_specs=in_specs, out_specs=rows, check_vma=False)
```

```python
import jax
import jax.numpy as jnp
from jax import lax
from jax.experimental import pallas as pl
from jax.experimental.pallas import tpu as pltpu
from jax.sharding import PartitionSpec as P

F32, BF16, I32 = jnp.float32, jnp.bfloat16, jnp.int32
N, NZ, NY = 32, 8, 4
CAP, LIVE = 40, 768
D, DO, FF = 7168, 3584, 288
HOLD = 28
PW, OW = 256, 128
HALF = LIVE // 2
FP = 384
T1 = 448
T2 = LIVE - T1
H1, H2 = T1 // 2, T2 // 2
S1 = 448
S2 = LIVE - S1
K1, K2 = S1 // 2, S2 // 2
HELD = tuple(d for d in range(N) if d % 9)
OROW = 48
ORDER = (4, 3, -3, 2, -2, 1, -1, 0)

ARRIVALS = (
    ("z1", 1, 0, 1), ("z1", 0, 0, 0), ("y2", 1, 0), ("z1", 0, 0, 1), ("y2", 0, 0), ("z1", 0, 1, 0), ("z1", 1, 1, 1),
    ("y1", 0, -1, 0, 0), ("y1", 1, 0, 0, 0), ("y1", 0, 0, 0, 1), ("z1", 1, 0, 0), ("y1", 1, -1, 0, 1),
    ("y1", 1, -1, 0, 0), ("y2", 0, 1), ("y2", 1, 1), ("z1", 0, 1, 1), ("z1", 1, 2, 1), ("y1", 1, 2, 0, 1),
    ("z2", 0, 0, 1), ("y1", 1, 1, 0, 1), ("z2", 1, 0, 0), ("z1", 1, 1, 0), ("y1", 0, 1, 0, 1), ("z2", 0, 0, 3),
    ("y1", 0, 0, 0, 0), ("z2", 1, 0, 3), ("z1", 1, 3, 1), ("z2", 0, 0, 0), ("z2", 1, 0, 2), ("y1", 0, -2, 0, 1),
    ("y1", 1, 0, 0, 1), ("z2", 0, 0, 2), ("z1", 0, 2, 1), ("y1", 0, -1, 1, 0), ("z1", 0, 2, 0), ("y1", 0, 1, 0, 0),
    ("z2", 1, 0, 1), ("z1", 1, 2, 0), ("z2", 0, 1, 1), ("z2", 1, 1, 0), ("z2", 1, 1, 2), ("z2", 0, 1, 0),
    ("y1", 0, 2, 0, 0), ("y1", 0, 4, 0, 1), ("z2", 0, 1, 3), ("y1", 1, -2, 0, 1), ("y1", 1, 2, 0, 0),
    ("y1", 0, -2, 0, 0), ("y1", 0, -1, 0, 1), ("z2", 1, 1, 1), ("y1", 0, 3, 0, 1), ("y1", 1, -1, 1, 1),
    ("y1", 1, 2, 1, 1), ("z2", 1, 1, 3), ("z2", 0, 1, 2), ("z1", 0, 3, 0), ("y1", 1, -3, 0, 1), ("z2", 0, 2, 1),
    ("y1", 1, -2, 0, 0), ("y1", 1, 0, 1, 1), ("y1", 0, 3, 0, 0), ("y1", 0, 0, 1, 0), ("y1", 0, 2, 1, 0),
    ("y1", 1, 3, 0, 0), ("y1", 1, 3, 0, 1), ("y1", 1, 4, 0, 1), ("y1", 1, -2, 1, 1), ("z2", 1, 2, 0),
    ("y1", 0, 2, 0, 1), ("y1", 1, -3, 0, 0), ("z2", 0, 2, 0), ("y1", 0, -3, 0, 0), ("y1", 0, -2, 1, 0),
    ("z2", 1, 2, 1), ("y1", 1, 1, 0, 0), ("y1", 0, 1, 1, 0), ("y1", 0, 4, 0, 0), ("z2", 0, 2, 3), ("z2", 1, 2, 2),
    ("y1", 1, 1, 1, 1), ("y1", 0, 3, 1, 0), ("z2", 0, 2, 2), ("z2", 1, 2, 3), ("z2", 0, 3, 1), ("y1", 1, 3, 1, 1),
    ("y1", 1, 4, 0, 0), ("z2", 0, 3, 0), ("y1", 0, -3, 0, 1), ("z2", 1, 3, 0), ("y1", 1, 4, 1, 1),
    ("y1", 0, -3, 1, 0), ("z2", 1, 3, 1), ("y1", 1, -3, 1, 1), ("y1", 0, 4, 1, 0), ("z2", 0, 3, 3), ("z2", 0, 3, 2),
    ("z2", 1, 3, 2), ("z2", 1, 3, 3),
)

SUMS = (
    ("tz", 1, 3, 1), ("tz", 0, 3, 1), ("tz", 0, 3, 2), ("tz", 1, 3, 2), ("tz", 1, 3, 3), ("ya", 1, 4), ("ya", 0, 4),
    ("tz", 1, 3, 0), ("tz", 0, 3, 0), ("tz", 0, 3, 3), ("ya", 0, 3), ("ya", 0, -3), ("tz", 1, 2, 1), ("tz", 0, 2, 1),
    ("tz", 0, 2, 2), ("ya", 1, -3), ("ya", 1, 3), ("ya", 1, -2), ("tz", 1, 2, 2), ("tz", 0, 2, 0), ("tz", 1, 2, 3),
    ("line", 4), ("tz", 1, 2, 0), ("ya", 1, 2), ("ya", 0, 2), ("tz", 0, 2, 3), ("tz", 0, 1, 2), ("tz", 1, 1, 2),
    ("ya", 0, -2), ("line", 3), ("line", -3), ("ya", 1, -1), ("tz", 0, 1, 3), ("tz", 1, 1, 1), ("tz", 0, 1, 1),
    ("ya", 1, 1), ("ya", 0, -1), ("ya", 0, 1), ("tz0", 2), ("tz", 1, 1, 3), ("ya", 1, 0), ("line", 2), ("line", -2),
    ("tz", 1, 1, 0), ("ya", 0, 0), ("tz", 0, 1, 0), ("tz0", 3), ("tz0", 1), ("line", 1), ("line", -1), ("tz0", 0),
    ("fin",), ("line", 0),
)


def kernel(
    counts, tv_h, ts_h, gv_h, gs_h, uv_h, us_h, dv_h, ds_h, out,
    tv, ts, gv, gs, gst, uv, us, ust, dv, ds, dst, asrc, adst, xs, onehot, back, w, wd, acc, hid, ring,
    r1, r2, yz, zr, tz, ty, far, res, osrc, odst,
    ld, a_s, a_r, z1_s, z1_r, y1_s, y1_r, y2_s, y2_r, z2_s, z2_r, s1, q1, s2, q2, sz, qz, st, qt, sy, qy, o_s, o_r,
):
    rep = lax.axis_index("replica")
    g = lax.axis_index("group")
    z, y = g // NY, g % NY
    up_y, dn_y = z * NY + (y + 1) % NY, z * NY + (y + 3) % NY
    up_z, dn_z = ((z + 1) % NZ) * NY + y, ((z + 7) % NZ) * NY + y
    def holds(dev):
        return dev % 9 != 0

    def piece_of(dev):
        return jnp.maximum(dev - 1 - dev // 9, 0)

    is_holder = holds(g)
    mine = piece_of(g)

    def remote(src, dst, send, recv, to):
        return pltpu.make_async_remote_copy(
            src, dst, send, recv, device_id=(rep, to), device_id_type=pl.DeviceIdType.MESH
        )

    loads = [
        pltpu.make_async_copy(a, b, ld.at[i])
        for i, (a, b) in enumerate(
            ((tv_h, tv), (ts_h, ts), (gv_h, gv), (gs_h, gst), (uv_h, uv), (us_h, ust), (dv_h, dv), (ds_h, dst))
        )
    ]
    for load in loads:
        load.start()
    barrier = pltpu.get_barrier_semaphore()

    def greet(i, c):
        pl.semaphore_signal(barrier, inc=1, device_id=(rep, (g + i) % N), device_id_type=pl.DeviceIdType.MESH)
        return c

    lax.fori_loop(1, N, greet, 0)

    loads[0].wait()
    loads[1].wait()
    tsf = ts[...].astype(F32)
    for p in range(HOLD):
        lo = tv[:, PW * p : PW * p + 128].astype(F32) * tsf[:, 2 * p : 2 * p + 1]
        hi = tv[:, PW * p + 128 : PW * p + 256].astype(F32) * tsf[:, 2 * p + 1 : 2 * p + 2]
        asrc[p] = jnp.concatenate([lo, hi], axis=0).astype(BF16)
    pl.semaphore_wait(barrier, N - 1)

    def far_first(i):
        k = i // NY
        dz = 4 + (k + 1) // 2 * (1 - 2 * (k % 2))
        return ((z + dz) % NZ) * NY + (y + i) % NY

    def scatter(i, c):
        to = far_first(i)

        @pl.when(holds(to) & (to != g))
        def _():
            remote(asrc.at[piece_of(to)], adst.at[g], a_s, a_r, to).start()

        return c

    lax.fori_loop(0, N, scatter, 0)

    offs, off = [], jnp.int32(0)
    lane = lax.broadcasted_iota(I32, (16, N * CAP), 1)
    target = jnp.full((16, N * CAP), -1, I32)
    for i in range(N):
        c = counts[i]
        rel = lane - CAP * i
        target = jnp.where((rel >= 0) & (rel < c), rel + off, target)
        offs.append(off)
        off = off + c
    row16 = lax.broadcasted_iota(I32, (16, N * CAP), 0)

    def build(r, c):
        hit = target == row16 + r * 16
        onehot[pl.ds(pl.multiple_of(r * 16, 16), 16), :] = jnp.where(hit, 1.0, 0.0).astype(BF16)
        return c

    lax.fori_loop(0, LIVE // 16, build, 0)

    for v, s, st_, at in ((gv, gs, gst, 0), (uv, us, ust, FP)):
        loads[2 if at == 0 else 4].wait()
        loads[3 if at == 0 else 5].wait()
        s[...] = st_[...].T

        def deq(r, c, v=v, s=s, at=at):
            r0 = pl.multiple_of(r * 32, 32)
            sf = s[pl.ds(r0, 32), :]
            for b in range(D // 128):
                val = v[pl.ds(r0, 32), 128 * b : 128 * b + 128].astype(F32) * sf[:, b : b + 1]
                w[b // 2, pl.ds(at + r0, 32), 128 * (b % 2) : 128 * (b % 2) + 128] = val.astype(BF16)
            return c

        lax.fori_loop(0, FF // 32, deq, 0)

    loads[6].wait()
    loads[7].wait()
    ds[...] = dst[...].T

    def deq_down(r, c):
        r0 = pl.multiple_of(r * 32, 32)
        sf = ds[pl.ds(r0, 32), :]
        for b in range(HOLD):
            val = dv[pl.ds(r0, 32), 128 * b : 128 * b + 128].astype(F32) * sf[:, b : b + 1]
            zz, yy = HELD[b] // NY, HELD[b] % NY
            i = zz - int(zz > 2 * yy)
            wd[yy, pl.ds(r0, 32), 128 * i : 128 * i + 128] = val.astype(BF16)
        return c

    lax.fori_loop(0, FF // 32, deq_down, 0)
    wd[:, FF:, :] = jnp.zeros((NY, FP - FF, DO // NY), BF16)

    def pad(p, c):
        w[p, FF:FP, :] = jnp.zeros((FP - FF, PW), BF16)
        w[p, FP + FF :, :] = jnp.zeros((FP - FF, PW), BF16)
        return c

    lax.fori_loop(0, HOLD, pad, 0)
    acc[...] = jnp.zeros_like(acc)

    jrow = lax.broadcasted_iota(I32, (OROW, LIVE), 0)
    diff = lax.broadcasted_iota(I32, (OROW, LIVE), 1) - jrow
    for i in range(N):
        hit = (diff == offs[i]) & (jrow < counts[i])
        back[i * OROW : (i + 1) * OROW, :] = jnp.where(hit, 1.0, 0.0).astype(BF16)

    @pl.when(is_holder)
    def _():
        adst[g] = asrc[mine]
        pltpu.make_async_copy(adst.at[pl.ds(0, N - 1)], adst.at[pl.ds(0, N - 1)], a_r).wait()

        def spread(k, c):
            a = adst[2 * k].astype(F32)
            b = adst[2 * k + 1].astype(F32)
            rows = pl.ds(pl.multiple_of(k * 80, 16), 80)
            xs[rows, 0:128] = jnp.concatenate([a[:CAP], b[:CAP]], axis=0).astype(BF16)
            xs[rows, 128:256] = jnp.concatenate([a[CAP:], b[CAP:]], axis=0).astype(BF16)
            return c

        lax.fori_loop(0, N // 2, spread, 0)

    def multiply(src, r0, n):
        acc[r0 : r0 + n, :] += lax.dot_general(
            ring[src, r0 : r0 + n, :], w[src], (((1,), (1,)), ((), ())), preferred_element_type=F32
        )

    def at(dz, dy):
        dev = ((z + dz + 8) % NZ) * NY + (y + dy + 4) % NY
        return holds(dev), piece_of(dev)

    def when(dz, dy, f):
        live, p = at(dz, dy)
        pl.when(live)(lambda: f(p))

    to_z, to_y = (up_z, dn_z), (up_y, dn_y)

    def over(ref, sem):
        pltpu.make_async_copy(ref, ref, sem).wait()

    def gathered():
        for way in range(2):
            for step in range(4):
                n1, n2 = (T1, T2) if step < 3 else (H1, H2)
                when(-sgn(way) * step, 0, lambda p: over(ring.at[0, 0:n1, :], z1_s.at[way, step]))
                whole = (z + step) % 2 == 1
                pl.when(whole)(lambda: over(ring.at[0:NY, 0:n2, :], z2_s.at[way, step]))
                pl.when(jnp.logical_not(whole))(lambda: over(ring.at[0 : NY - 1, 0:n2, :], z2_s.at[way, step]))
            over(ring.at[0:7, 0 : T1 + H1, :], y1_s.at[way])
            when(0, 0, lambda p: y2(way, 0, p).wait_send())
            when(0, -sgn(way), lambda p: y2(way, 1, p).wait_send())

    def sgn(way):
        return 1 - 2 * way

    def z1(way, step, half, p):
        ref = ring.at[p, pl.ds(half * H1, H1), :]
        return remote(ref, ref, z1_s.at[way, step], z1_r.at[way, step, half], to_z[way])

    def y1(way, e, step, half, p):
        ref = ring.at[p, pl.ds(half * H1, H1), :]
        i = e % NZ
        return remote(ref, ref, y1_s.at[way], y1_r.at[way, i, half if step == 0 else 2], to_y[way])

    def y2(way, step, p):
        ref = ring.at[p, pl.ds(T1, T2), :] if step == 0 else ring.at[p, pl.ds(T1 + way * H2, H2), :]
        return remote(ref, ref, y2_s.at[way, step], y2_r.at[way, step], to_y[way])

    def z2(way, step, dy, p):
        ref = ring.at[p, pl.ds(T1, T2), :] if step < 3 else ring.at[p, pl.ds(T1 + way * H2, H2), :]
        return remote(ref, ref, z2_s.at[way, step], z2_r.at[way, step, dy], to_z[way])

    def y1_send(e, half):
        def f(p):
            for way in range(2):
                y1(way, e, 0, half, p).start()

        when(e, 0, f)

    def z2_send(dy):
        def f(p):
            for way in range(2):
                z2(way, 0, dy, p).start()

        when(0, dy, f)

    def take_z1(way, step, half):
        d = step + 1

        def f(p):
            z1(way, step, half, p).wait_recv()
            if d < 3 or (d == 3 and half == way):
                z1(way, d, half, p).start()

        when(-sgn(way) * d, 0, f)
        y1_send(-sgn(way) * d, half)

    def take_y1(way, e, step, half):
        def f(p):
            y1(way, e, step, half, p).wait_recv()
            if step == 0 and half == way:
                y1(way, e, 1, half, p).start()

        when(e, -sgn(way) * (step + 1), f)

    def take_y2(way, step):
        def f(p):
            y2(way, step, p).wait_recv()
            if step == 0:
                y2(way, 1, p).start()

        when(0, -sgn(way) * (step + 1), f)
        if step == 0:
            z2_send(-sgn(way) % NY)
        elif way == 1:
            z2_send(2)

    def take_z2(way, step, dy):
        d = step + 1

        def f(p):
            z2(way, step, dy, p).wait_recv()
            if d < 4:
                z2(way, d, dy, p).start()

        when(-sgn(way) * d, dy, f)

    takes = {"z1": take_z1, "y1": take_y1, "y2": take_y2, "z2": take_z2}

    def column(e, lo, hi):
        def body(i, c):
            when(e, jnp.where(i < 2, i, 5 - i), lambda p: multiply(p, 0, T1))
            return c

        lax.fori_loop(lo, hi, body, 0)

    def ring_of(d):
        def body(i, c):
            dz = d if d in (0, 4) else jnp.where(i < NY, d, -d)
            when(dz, i % NY, lambda p: multiply(p, T1, T2))
            return c

        lax.fori_loop(0, NY if d in (0, 4) else 2 * NY, body, 0)

    def slab(dy):
        yy = (y + dy) % NY
        for r in range(4):
            rows = pl.ds(r * 192, 192)
            got = jnp.dot(hid[rows, :], wd[yy], preferred_element_type=F32).astype(BF16)
            for i in range(7):
                zz = i + (i >= 2 * yy).astype(I32)
                w[piece_of(zz * NY + yy), rows, 0:OW] = got[:, i * OW : (i + 1) * OW]

    def slab_far(dy):
        yy, zz = (y + dy) % NY, (z + 4) % NZ
        i = zz - (zz > 2 * yy).astype(I32)
        cols = wd[yy, :, pl.ds(pl.multiple_of(i * OW, OW), OW)]
        far[dy] = jnp.dot(hid[S1:, :], cols, preferred_element_type=F32).astype(BF16)

    def part(p, r0, n):
        return w.at[p, r0 : r0 + n, 0:OW]

    def m1(way, e, p):
        return remote(part(p, way * K1, K1), r1.at[way, e % NZ], s1.at[way], q1.at[way, e % NZ], to_y[way])

    def m2(way, e, p):
        return remote(part(p, 0, S1), r2.at[way, e % NZ], s2.at[way], q2.at[e % NZ], to_y[way])

    def mz(way, dist):
        e = sgn(way) * dist % NZ
        if dist == 4:
            rows = pl.ds(way * K1, K1)
            return remote(yz.at[e, rows, :], zr.at[way, 3, rows, :], sz.at[way, 3], qz.at[way, 3], to_z[way])
        return remote(yz.at[e], zr.at[way, dist - 1], sz.at[way, dist - 1], qz.at[way, dist - 1], to_z[way])

    def mt(way, dist, dy, p):
        if dist == 4:
            rows = pl.ds(way * K2, K2)
            src, dst = far.at[dy, rows, :], tz.at[way, 3, dy, rows, :]
        else:
            src, dst = part(p, S1, S2), tz.at[way, dist - 1, dy]
        return remote(src, dst, st.at[way, dist - 1], qt.at[way, dist - 1, dy], to_z[way])

    def my(dy, p):
        to = z * NY + (y + dy) % NY
        return remote(part(p, S1, S2), ty.at[dy - 1], sy.at[dy - 1], qy.at[dy - 1], to)

    def add(ref, *others):
        total = ref[...].astype(F32)
        for other in others:
            total = total + other.astype(F32)
        return total

    def sum_ya(way, e):
        def f(p):
            m1(way, e, p).wait_recv()
            ref = part(p, way * K1, K1)
            ref[...] = add(ref, r1[way, e % NZ]).astype(BF16)
            m2(way, e, p).start()

        when(e, sgn(way), f)

    def sum_line(e):
        ways = {4: (), 0: (0, 1)}.get(e, (0,) if e > 0 else (1,))

        def f(p):
            over(r2.at[:, e % NZ], q2.at[e % NZ])
            for way in ways:
                mz(way, abs(e) + 1).wait_recv()
            for h in range(2):
                rows = pl.ds(h * K1, K1)
                more = [zr[way, abs(e), rows, :] for way in ways if abs(e) < 3 or way == h]
                total = add(part(p, h * K1, K1), r2[0, e % NZ, rows, :], r2[1, e % NZ, rows, :], *more)
                if e == 0:
                    res[rows, :] = total.astype(BF16)
                else:
                    yz[e % NZ, rows, :] = total.astype(BF16)
            if e == 4:
                mz(0, 4).start()
                mz(1, 4).start()
            elif e != 0:
                mz(ways[0], abs(e)).start()

        when(e, 0, f)

    def sum_tz(way, d, dy):
        def f(p):
            mt(way, d + 1, dy, p).wait_recv()
            if d == 3:
                ref, got = part(p, S1 + way * K2, K2), tz[way, 3, dy, pl.ds(way * K2, K2), :]
            else:
                ref, got = part(p, S1, S2), tz[way, d, dy]
            ref[...] = add(ref, got).astype(BF16)
            mt(way, d, dy, p).start()

        when(sgn(way) * d, dy, f)

    def sum_tz0(dy):
        def f(p):
            for way in range(2):
                mt(way, 1, dy, p).wait_recv()
            ref = part(p, S1, S2)
            ref[...] = add(ref, tz[0, 0, dy], tz[1, 0, dy]).astype(BF16)
            if dy:
                my(dy, p).start()

        when(0, dy, f)

    def sum_fin():
        def f(p):
            for dy in range(1, NY):
                my(dy, p).wait_recv()
            res[S1:, :] = add(part(p, S1, S2), ty[0], ty[1], ty[2]).astype(BF16)

        when(0, 0, f)

    sums = {"ya": sum_ya, "line": sum_line, "tz": sum_tz, "tz0": sum_tz0, "fin": sum_fin}
    def hidden(lo, hi):
        for r in range(lo, hi, 64):
            rows = pl.ds(r, 64)
            gate = acc[rows, 0:FP]
            hid[rows, :] = (gate / (1.0 + jnp.exp(-gate)) * acc[rows, FP : 2 * FP]).astype(BF16)

    def start_far():
        for dy in range(NY):
            slab_far(dy)
        for dy in range(NY):

            def f(p, dy=dy):
                mt(0, 4, dy, p).start()
                mt(1, 4, dy, p).start()

            when(4, dy, f)

    @pl.when(is_holder)
    def _():
        for h in range(2):
            ring[mine, pl.ds(h * HALF, HALF), :] = jnp.dot(
                onehot[pl.ds(h * HALF, HALF), :], xs[...], preferred_element_type=F32
            ).astype(BF16)
        for way in range(2):
            y2(way, 0, mine).start()
        for i in range(2):
            for way in range(2):
                z1(way, 0, i if way == 0 else 1 - i, mine).start()

    y1_send(0, 0)
    y1_send(0, 1)
    z2_send(0)
    for n, (wave, *which) in enumerate(ARRIVALS):
        takes[wave](*which)
        later = ARRIVALS[n + 1 :]
        if wave == "z2" and not any(o[0] == "z2" and o[2] == which[1] for o in later):
            ring_of(which[1] + 1)
            if which[1] == 3:
                hidden(T1, LIVE)
                start_far()
        if wave == "y2" and not any(o[0] == "y2" for o in later):
            ring_of(0)
        if wave == "y1" and not any(o[0] == "y1" and o[2] == which[1] for o in later):
            column(which[1], 3 if which[1] == 4 else 0, 4)
        if wave == "y1" and which[1:3] == [4, 0] and not any(o[0] == "y1" and o[2:4] == (4, 0) for o in later):
            column(4, 0, 3)

    hidden(0, T1)
    slab(2)
    for e in ORDER:

        def f(p, e=e):
            m1(0, e, p).start()
            m1(1, e, p).start()

        when(e, 2, f)
    slab(1)
    slab(3)
    slab(0)
    for n, (wave, *which) in enumerate(SUMS):
        if n == len(SUMS) // 2:
            gathered()
        sums[wave](*which)

    @pl.when(is_holder)
    def _():
        for h in range(4):
            slots = jnp.dot(back[h * 384 : (h + 1) * 384, :], res[...], preferred_element_type=F32).astype(BF16)
            for i in range(8):
                osrc[8 * h + i] = slots[i * OROW : (i + 1) * OROW]
        odst[mine] = osrc[g]

        def give(i, c):
            to = far_first(i)

            @pl.when(to != g)
            def _():
                remote(osrc.at[to], odst.at[mine], o_s, o_r, to).start()

            return c

        lax.fori_loop(0, N, give, 0)

    for way in range(2):
        over(r1.at[way, 0:7], s1.at[way])
        over(r2.at[way, 0:7], s2.at[way])
        for dist in range(1, 5):
            when(sgn(way) * dist, 0, lambda p: mz(way, dist).wait_send())
            n2 = S2 if dist < 4 else K2
            whole = (z + dist) % 2 == 1
            pl.when(whole)(lambda: over(tz.at[way, 0, :, 0:n2, :], st.at[way, dist - 1]))
            pl.when(jnp.logical_not(whole))(lambda: over(tz.at[way, 0, 0 : NY - 1, 0:n2, :], st.at[way, dist - 1]))

    for dy in range(1, NY):
        when(0, dy, lambda p: my(dy, p).wait_send())

    @pl.when(is_holder)
    def _():
        over(asrc.at[0 : HOLD - 1], a_s)
        over(odst.at[0 : HOLD - 1], o_r)
        over(osrc.at[0 : N - 1], o_s)

    @pl.when(jnp.logical_not(is_holder))
    def _():
        over(asrc.at[0:HOLD], a_s)
        over(odst.at[0:HOLD], o_r)

    for p in range(HOLD):
        out[:, p * OW : (p + 1) * OW] = odst[p][:CAP]


def shards(tv, ts, counts, gv, gs, uv, us, dv, ds):
    any_space = pl.BlockSpec(memory_space=pl.ANY)
    vmem, dma = pltpu.VMEM, pltpu.SemaphoreType.DMA
    return pl.pallas_call(
        kernel,
        out_shape=jax.ShapeDtypeStruct((CAP, DO), BF16),
        in_specs=[pl.BlockSpec(memory_space=pltpu.SMEM)] + [any_space] * 8,
        out_specs=pl.BlockSpec(memory_space=pltpu.VMEM),
        scratch_shapes=[
            vmem((CAP, D), BF16),
            vmem((CAP, D // 128), BF16),
            vmem((FF, D), BF16),
            vmem((FF, D // 128), F32),
            vmem((D // 128, FF), F32),
            vmem((FF, D), BF16),
            vmem((FF, D // 128), F32),
            vmem((D // 128, FF), F32),
            vmem((FF, DO), BF16),
            vmem((FF, DO // 128), F32),
            vmem((DO // 128, FF), F32),
            vmem((HOLD, 2 * CAP, 128), BF16),
            vmem((N, 2 * CAP, 128), BF16),
            vmem((N * CAP, PW), BF16),
            vmem((LIVE, N * CAP), BF16),
            vmem((N * OROW, LIVE), BF16),
            vmem((HOLD, 2 * FP, PW), BF16),
            vmem((NY, FP, DO // NY), BF16),
            vmem((LIVE, 2 * FP), F32),
            vmem((LIVE, FP), BF16),
            vmem((HOLD, LIVE, PW), BF16),
            vmem((2, 8, K1, OW), BF16),
            vmem((2, 8, S1, OW), BF16),
            vmem((8, S1, OW), BF16),
            vmem((2, 4, S1, OW), BF16),
            vmem((2, 4, NY, S2, OW), BF16),
            vmem((3, S2, OW), BF16),
            vmem((NY, S2, OW), BF16),
            vmem((LIVE, OW), BF16),
            vmem((N, OROW, OW), BF16),
            vmem((HOLD, OROW, OW), BF16),
            dma((8,)),
            dma,
            dma,
            dma((2, 4)),
            dma((2, 4, 2)),
            dma((2,)),
            dma((2, NZ, 3)),
            dma((2, 2)),
            dma((2, 2)),
            dma((2, 4)),
            dma((2, 4, NY)),
            dma((2,)),
            dma((2, 8)),
            dma((2,)),
            dma((8,)),
            dma((2, 4)),
            dma((2, 4)),
            dma((2, 4)),
            dma((2, 4, NY)),
            dma((3,)),
            dma((3,)),
            dma,
            dma,
        ],
        compiler_params=pltpu.CompilerParams(
            collective_id=0, has_side_effects=True, vmem_limit_bytes=60 * 2**20
        ),
        cost_estimate=pl.CostEstimate(flops=10**10, bytes_accessed=12 * 10**6, transcendentals=LIVE * FF),
        name="swiglu",
    )(counts, tv, ts, gv, gs.T, uv, us.T, dv, ds.T)


def solution(mesh):
    rows, split = P(("replica", "group"), None), P("group", None)
    in_specs = (rows, rows, P("replica")) + (split,) * 6
    return jax.shard_map(shards, mesh=mesh, in_specs=in_specs, out_specs=rows, check_vma=False)
```
